512 devices in a mesh: gx: 16 (over z, x_lo), gy: 32 (over y, x_hi, core).
Axes of the slice: x: 4 (x_hi: 2, x_lo: 2; x = x_hi * 2 + x_lo), y: 8, z: 8, core: 2. Of those that a mesh axis runs over, the one named last changes fastest.
Arguments:
- vectors: bfloat16 [2048, 32, 256], P(('gx', 'gy')), may hold values from -6 to 6
- leaf_basis: bfloat16 [2048, 256, 64], P(('gx', 'gy')), may hold values from -0.375 to 0.375
- near_blocks: bfloat16 [2048, 3, 256, 256], P(('gx', 'gy')), may hold values from -0.21875 to 0.21875
- near_index: int32 [2048, 3], P(('gx', 'gy')), may hold values from 0 to 2047, as said below
- near_count: int32 [2048], P(('gx', 'gy')), may hold values from 1 to 3, as said below
- leaf_couple: bfloat16 [2048, 6, 64, 64], P(('gx', 'gy')), may hold values from -0.3125 to 0.3125
- far_index: int32 [2048, 6], P(('gx', 'gy')), may hold values from 0 to 2047, as said below
- leaf_transfer: bfloat16 [2048, 64, 64], P(('gx', 'gy')), may hold values from -0.375 to 0.375
- level_couple: bfloat16 [3, 512, 4, 64, 64], P(None, ('gx', 'gy')), as said below
- level_transfer: bfloat16 [2, 512, 64, 64], P(None, ('gx', 'gy')), as said below
Outputs:
- result_field: float32 [2048, 32, 256], P(('gx', 'gy'))
The draws below stay inside these ranges and needn't reach their ends.
Inputs may be any that keep to these rules, and one draw needn't show every extreme that they name: |near_index[t, j] - t| <= 8 for every leaf t, and this bound is reached. Slots j >= near_count[t] are padding; every device has a leaf with all 3 slots live. |far_index[t, j] - t| <= 8 for every leaf t, and this bound is reached. level_couple[k, a] equals level_couple[k, b] when a and b lie in one cluster of level k. level_transfer[k, a] equals level_transfer[k, b] when a and b lie in one cluster of level k.
All inputs are finite; a program needn't handle non-finite values.
Results may differ from the reference program's by a relative error of at most 0.0025.
Values may be sent and summed in bfloat16 or wider, within the bound.
A program may use at most 128 MiB of HBM per device.

```python
import jax
import jax.numpy as jnp
from jax import lax

LEAF = 256
RANK = 64
RHS = 32
LD = 4
NEAR = 3
FARL = 6
UPL = 3
DEVICE_NODES = 512
LEAVES = 2048


def partner_leaves(key, slots):
    leaf_ids = jnp.arange(LEAVES, dtype=jnp.int32)[:, None]
    reach_leaves = 2 * LD
    shifts_drawn = jax.random.randint(key, (LEAVES, slots), -reach_leaves, reach_leaves + 1, dtype=jnp.int32)
    position = leaf_ids % LD
    first_column = jnp.where(position[:, 0] == 0, -reach_leaves, jnp.where(position[:, 0] == LD - 1, reach_leaves, shifts_drawn[:, 0]))
    shifts_drawn = shifts_drawn.at[:, 0].set(first_column)
    return jnp.clip(leaf_ids + shifts_drawn, 0, LEAVES - 1).astype(jnp.int32)


def node_copies(drawn, levels):
    height = jnp.arange(levels, dtype=jnp.int32)[:, None]
    stride = jnp.power(2, height)
    source = jnp.arange(DEVICE_NODES, dtype=jnp.int32)[None, :] // stride * stride
    return drawn[height, source]


def draw_near_index(key, part):
    key = jax.random.fold_in(key, 3)
    return partner_leaves(key, NEAR)


def draw_far_index(key, part):
    key = jax.random.fold_in(key, 5)
    return partner_leaves(key, FARL)


def draw_near_count(key, part):
    key = jax.random.fold_in(key, 9)
    counts = jax.random.randint(key, (LEAVES,), 1, NEAR + 1, dtype=jnp.int32)
    position = jnp.arange(LEAVES, dtype=jnp.int32) % LD
    return jnp.where(position == 0, NEAR, counts).astype(jnp.int32)


def draw_level_couple(key, part):
    key = jax.random.fold_in(key, 7)
    drawn = jax.random.normal(key, (UPL, DEVICE_NODES, 4, RANK, RANK), jnp.float32) * (4.0 * RANK) ** (-0.5)
    return node_copies(drawn, UPL).astype(jnp.bfloat16)


def draw_level_transfer(key, part):
    key = jax.random.fold_in(key, 11)
    drawn = jax.random.normal(key, (UPL - 1, DEVICE_NODES, RANK, RANK), jnp.float32) * (2.0 * RANK) ** (-0.5)
    return node_copies(drawn, UPL - 1).astype(jnp.bfloat16)


def shard_levels(stream_key, shape, pieces, smallest, top_value):
    gain = 1.0
    for dim, shards_of in pieces:
        steps = jax.random.uniform(jax.random.fold_in(jax.random.fold_in(stream_key, 6), dim), (shards_of,), jnp.float32, smallest / len(pieces), top_value / len(pieces))
        gain = gain * jnp.repeat(jnp.exp(steps), shape[dim] // shards_of).reshape((-1,) + (1,) * (len(shape) - 1 - dim))
    return gain


def gaussian(own_key, dims, width, most, shards=(), held_as=jnp.bfloat16):
    level = shard_levels(own_key, dims, shards, -0.22, 0.18) if shards else 1.0
    array = jax.random.normal(own_key, dims, jnp.float32) * width * level
    return jnp.minimum(jnp.maximum(array, -most), most).astype(held_as)


def setup_inputs(seed: int = 0) -> dict:
    splits = jax.random.split(jax.random.key(seed), 11)
    vectors = gaussian(splits[0], (LEAVES, RHS, LEAF), 1.0, 6.0, ((0, 512),))
    leaf_basis = gaussian(splits[1], (LEAVES, LEAF, RANK), LEAF ** -0.5, 0.375, ((0, 512),))
    near_blocks = gaussian(splits[2], (LEAVES, NEAR, LEAF, LEAF), (LEAF * NEAR) ** -0.5, 0.21875, ((0, 512),))
    near_index = draw_near_index(jax.random.fold_in(splits[10], 71), 0)
    near_count = draw_near_count(jax.random.fold_in(splits[10], 71), 0)
    leaf_couple = gaussian(splits[5], (LEAVES, FARL, RANK, RANK), (FARL * RANK) ** -0.5, 0.3125, ((0, 512),))
    far_index = draw_far_index(jax.random.fold_in(splits[10], 71), 0)
    leaf_transfer = gaussian(splits[7], (LEAVES, RANK, RANK), (RANK * LD) ** -0.5, 0.375, ((0, 512),))
    level_couple = draw_level_couple(jax.random.fold_in(splits[10], 71), 0)
    level_transfer = draw_level_transfer(jax.random.fold_in(splits[10], 71), 0)
    return dict(vectors=vectors, leaf_basis=leaf_basis, near_blocks=near_blocks, near_index=near_index, near_count=near_count, leaf_couple=leaf_couple, far_index=far_index, leaf_transfer=leaf_transfer, level_couple=level_couple, level_transfer=level_transfer)


node_offsets = (-3, -2, 2, 3)


def shift_nodes(values, offset):
    count_nodes = values.shape[0]
    if abs(offset) >= count_nodes:
        return jnp.zeros_like(values)
    filler = jnp.zeros((abs(offset),) + values.shape[1:], values.dtype)
    if offset > 0:
        return jnp.concatenate([values[offset:], filler], axis=0)
    return jnp.concatenate([filler, values[:offset]], axis=0)


def reference(vectors, leaf_basis, near_blocks, near_index, near_count, leaf_couple, far_index, leaf_transfer, level_couple, level_transfer):
    highest = lax.Precision.HIGHEST
    coefficients = jnp.einsum("trl,tlm->trm", vectors.astype(jnp.float32), leaf_basis.astype(jnp.float32), precision=highest).astype(jnp.bfloat16)
    grouped = coefficients.astype(jnp.float32).reshape(DEVICE_NODES, LD, RHS, RANK)
    transfers = leaf_transfer.astype(jnp.float32).reshape(DEVICE_NODES, LD, RANK, RANK)
    upward = jnp.einsum("dlrm,dlmn->drn", grouped, transfers, precision=highest)
    ups = []
    for height in range(UPL):
        ups.append(upward)
        if height < UPL - 1:
            mats = level_transfer[height, :: 2 ** height].astype(jnp.float32)
            contrib = jnp.einsum("nrm,nmp->nrp", upward, mats, precision=highest)
            upward = contrib[0::2] + contrib[1::2]
    downs = []
    for height in range(UPL):
        current = ups[height]
        mats = level_couple[height, :: 2 ** height].astype(jnp.float32)
        total = jnp.zeros_like(current)
        for slot_id, offset in enumerate(node_offsets):
            shifted = shift_nodes(current, offset)
            total = total + jnp.einsum("nrm,nmp->nrp", shifted, mats[:, slot_id], precision=highest)
        downs.append(total)
    far_field = downs[UPL - 1]
    for height in reversed(range(UPL - 1)):
        mats = level_transfer[height, :: 2 ** height].astype(jnp.float32)
        parent_part = jnp.repeat(far_field, 2, axis=0)
        far_field = downs[height] + jnp.einsum("nrp,nmp->nrm", parent_part, mats, precision=highest)
    leaf_part = jnp.einsum("drp,dlmp->dlrm", far_field, transfers, precision=highest).reshape(LEAVES, RHS, RANK)
    partner_coeffs = coefficients[far_index].astype(jnp.float32)
    local_far = jnp.einsum("tjrm,tjmn->trn", partner_coeffs, leaf_couple.astype(jnp.float32), precision=highest)
    field = (leaf_part + local_far).astype(jnp.bfloat16)
    far_out = jnp.einsum("trm,tlm->trl", field.astype(jnp.float32), leaf_basis.astype(jnp.float32), precision=highest)

    def near_group(group):
        blocks, index_rows, counts = group
        picked = vectors[index_rows].astype(jnp.float32)
        live = jnp.arange(NEAR)[None, :] < counts[:, None]
        picked = jnp.where(live[:, :, None, None], picked, jnp.zeros((), jnp.float32))
        return jnp.einsum("tjrl,tjlk->trk", picked, blocks.astype(jnp.float32), precision=highest)

    near_part = lax.map(near_group, (near_blocks.reshape(DEVICE_NODES, LD, NEAR, LEAF, LEAF), near_index.reshape(DEVICE_NODES, LD, NEAR), near_count.reshape(DEVICE_NODES, LD)))
    return far_out + near_part.reshape(LEAVES, RHS, LEAF)
```

```python
import jax
import jax.numpy as jnp
from jax import lax
from jax.experimental import pallas as pl
from jax.experimental.pallas import tpu as pltpu
from jax.sharding import PartitionSpec as P

MESH = pl.DeviceIdType.MESH
NODES = 512
OFFSETS = (-3, -2, 2, 3)
NEAR_OFFSETS = (-2, -1, 1, 2)
F32, BF16 = jnp.float32, jnp.bfloat16


def split(x):
    high = x.astype(BF16)
    return high, (x - high.astype(F32)).astype(BF16)


def dot(a, b):
    return jnp.dot(a, b, preferred_element_type=F32)


def dot_t(a, b):
    return lax.dot_general(a, b, (((1,), (1,)), ((), ())), preferred_element_type=F32)


def twice(dot_fn, x, w):
    rows = x.shape[0]
    both = dot_fn(jnp.concatenate(split(x), axis=0), w)
    return both[:rows] + both[rows:]


def packed(x):
    x = x.astype(BF16)
    return jnp.concatenate([x[:16], x[16:]], axis=1)


def where_is(index):
    return (index // 32, lax.rem(index, 32))


def partners(me):
    out = []
    for level in (2, 1, 0):
        members = 2**level
        cluster, member = me // members, lax.rem(me, members)
        first = (0, 4, 12)[level]
        for slot, offset in enumerate(OFFSETS):
            for c in range(members):
                to = (cluster - offset) * members + c
                out.append((level, to, first + slot * members + member, (cluster + offset) * members + c, first + slot * members + c))
    return out


def kernel(
    near_index, near_count, far_index,
    vectors_hbm, basis_hbm, near_hbm, couple_hbm, transfer_hbm, lcouple_hbm, ltransfer_hbm,
    out_ref,
    window, basis, blocks, couple, transfer, lcouple, ltransfer,
    coeffs, doubled, ups, arrived, weights,
    load_sem, vec_send, vec_recv, coef_send, coef_recv, up_send, up_recv,
):
    me = lax.axis_index("gx") * 32 + lax.axis_index("gy")

    def inside(device):
        return jnp.logical_and(device >= 0, device < NODES)

    loads = [
        pltpu.make_async_copy(source, target, load_sem.at[i])
        for i, (source, target) in enumerate((
            (vectors_hbm, window.at[pl.ds(8, 4)]),
            (basis_hbm, basis),
            (transfer_hbm, transfer),
            (ltransfer_hbm, ltransfer),
            (lcouple_hbm, lcouple),
            (couple_hbm, couple),
            (near_hbm, blocks),
        ))
    ]
    for load in loads:
        load.start()

    far = partners(me)
    barrier = pltpu.get_barrier_semaphore()
    greeted = [me + d for d in NEAR_OFFSETS] + [p[1] for p in far]
    expected = jnp.int32(0)
    for device in greeted:
        there = inside(device)
        expected = expected + there.astype(jnp.int32)

        @pl.when(there)
        def _():
            pl.semaphore_signal(barrier, inc=1, device_id=where_is(device), device_id_type=MESH)

    for _, _, _, source, slot in far:
        @pl.when(jnp.logical_not(inside(source)))
        def _():
            arrived[slot] = jnp.zeros((16, 128), BF16)

    pl.semaphore_wait(barrier, expected)

    def vec_copy(i, d):
        return pltpu.make_async_remote_copy(
            src_ref=vectors_hbm, dst_ref=window.at[pl.ds((2 - d) * 4, 4)],
            send_sem=vec_send.at[i], recv_sem=vec_recv.at[3 - i],
            device_id=where_is(me + d), device_id_type=MESH)

    def coef_copy(i, d):
        return pltpu.make_async_remote_copy(
            src_ref=coeffs.at[2], dst_ref=coeffs.at[2 - d],
            send_sem=coef_send.at[i], recv_sem=coef_recv.at[3 - i],
            device_id=where_is(me + d), device_id_type=MESH)

    def up_copy(i):
        level, to, slot, _, _ = far[i]
        return pltpu.make_async_remote_copy(
            src_ref=ups.at[level], dst_ref=arrived.at[slot],
            send_sem=up_send.at[i], recv_sem=up_recv.at[slot],
            device_id=where_is(to), device_id_type=MESH)

    for i, d in enumerate(NEAR_OFFSETS):
        pl.when(inside(me + d))(vec_copy(i, d).start)

    for load in loads[:4]:
        load.wait()
    own = [dot(window[8 + t], basis[t]).astype(BF16) for t in range(4)]
    coefficients = jnp.concatenate(own, axis=1)
    coeffs[2] = coefficients
    up0 = dot(coefficients, transfer[...].reshape(256, 64))
    up1 = twice(dot, up0, ltransfer[0, 0])
    up2 = twice(dot, up1, ltransfer[1, 0])
    ups[0] = packed(up0)
    ups[1] = packed(up1)
    ups[2] = packed(up2)
    for i, p in enumerate(far):
        pl.when(inside(p[1]))(up_copy(i).start)
    for i, d in enumerate(NEAR_OFFSETS):
        pl.when(inside(me + d))(coef_copy(i, d).start)

    loads[4].wait()
    transfer_all = transfer[...].reshape(256, 64)
    step = lcouple[0, 0].reshape(256, 64)
    mats = [step.astype(F32)]
    mats.append(dot_t(lcouple[1, 0].reshape(256, 64), ltransfer[0, 0]))
    mats.append(twice(dot_t, dot_t(lcouple[2, 0].reshape(256, 64), ltransfer[1, 0]), ltransfer[0, 0]))
    for level in range(3):
        high, low = split(twice(dot_t, mats[level], transfer_all))
        weights[0, level] = high
        weights[1, level] = low

    lane = lax.broadcasted_iota(jnp.int32, (32, 128), 1)
    left = lane < 64
    left16 = left[:16]

    def level_part(level):
        members = 2**level
        first = (0, 4, 12)[level]
        sums = []
        for slot in range(4):
            total = arrived[first + slot * members].astype(F32)
            for c in range(1, members):
                total = total + arrived[first + slot * members + c].astype(F32)
            sums.append(total)
        parts = []
        for a, b in ((0, 1), (2, 3)):
            top = jnp.where(left16, sums[a], pltpu.roll(sums[b], 64, 1))
            low = jnp.where(left16, pltpu.roll(sums[a], 64, 1), sums[b])
            parts.append(jnp.concatenate([top, low], axis=0))
        high, low = split(jnp.concatenate(parts, axis=1))
        both = dot(jnp.concatenate([high, low], axis=0), weights[0, level])
        return both[:32] + both[32:] + dot(high, weights[1, level])

    def wait_level(level):
        first, count = ((0, 4), (4, 8), (12, 16))[level]
        for i, (_, _, _, source, slot) in enumerate(far):
            if first <= slot_of[i] < first + count:
                pl.when(inside(source))(
                    pltpu.make_async_remote_copy(
                        src_ref=ups.at[level], dst_ref=arrived.at[slot],
                        send_sem=up_send.at[i], recv_sem=up_recv.at[slot],
                        device_id=where_is(source), device_id_type=MESH).wait_recv)

    slot_of = [p[4] for p in far]

    for i, d in enumerate(NEAR_OFFSETS):
        pl.when(inside(me - d))(coef_copy(i, d).wait_recv)

    loads[5].wait()
    for block in range(5):
        for pair in range(2):
            two = coeffs[block, :, pl.ds(pair * 128, 128)].astype(F32)
            turned = pltpu.roll(two, 64, 1)
            doubled[block * 4 + pair * 2] = jnp.where(left, two, turned).astype(BF16)
            doubled[block * 4 + pair * 2 + 1] = jnp.where(left, turned, two).astype(BF16)
    base = (me - 2) * 4

    def place(leaf):
        return jnp.clip(leaf - base, 0, 19)

    local = []
    for t in range(4):
        cols = []
        for j in range(0, 6, 2):
            first = doubled[place(far_index[t, j])]
            second = doubled[place(far_index[t, j + 1])]
            cols.append(jnp.where(left, first, second))
        local.append(dot(jnp.concatenate(cols, axis=1), couple[t].reshape(384, 64)))
    field = jnp.concatenate(local, axis=1)

    wait_level(0)
    field = field + level_part(0)

    loads[6].wait()
    for i, d in enumerate(NEAR_OFFSETS):
        pl.when(inside(me - d))(vec_copy(i, d).wait_recv)
    for t in range(4):
        picked = []
        for j in range(3):
            rows = window[place(near_index[t, j])]
            picked.append(jnp.where(j < near_count[t], rows, jnp.zeros_like(rows)))
        out_ref[t] = dot(jnp.concatenate(picked, axis=1), blocks[t].reshape(768, 256))

    wait_level(1)
    field = field + level_part(1)
    for i, d in enumerate(NEAR_OFFSETS):
        pl.when(inside(me + d))(vec_copy(i, d).wait_send)
        pl.when(inside(me + d))(coef_copy(i, d).wait_send)
    for i, p in enumerate(far):
        pl.when(inside(p[1]))(up_copy(i).wait_send)
    wait_level(2)
    field = (field + level_part(2)).astype(BF16)
    for t in range(4):
        out_ref[t] = out_ref[t] + dot_t(field[:, t * 64:(t + 1) * 64], basis[t])


def on_device(vectors, leaf_basis, near_blocks, near_index, near_count, leaf_couple, far_index, leaf_transfer, level_couple, level_transfer):
    smem = pl.BlockSpec(memory_space=pltpu.SMEM)
    hbm = pl.BlockSpec(memory_space=pltpu.HBM)
    dma = pltpu.SemaphoreType.DMA
    return pl.pallas_call(
        kernel,
        out_shape=jax.ShapeDtypeStruct((4, 32, 256), F32),
        in_specs=[smem] * 3 + [hbm] * 7,
        out_specs=pl.BlockSpec(memory_space=pltpu.VMEM),
        scratch_shapes=[
            pltpu.VMEM((20, 32, 256), BF16),
            pltpu.VMEM((4, 256, 64), BF16),
            pltpu.VMEM((4, 3, 256, 256), BF16),
            pltpu.VMEM((4, 6, 64, 64), BF16),
            pltpu.VMEM((4, 64, 64), BF16),
            pltpu.VMEM((3, 1, 4, 64, 64), BF16),
            pltpu.VMEM((2, 1, 64, 64), BF16),
            pltpu.VMEM((5, 32, 256), BF16),
            pltpu.VMEM((20, 32, 128), BF16),
            pltpu.VMEM((3, 16, 128), BF16),
            pltpu.VMEM((28, 16, 128), BF16),
            pltpu.VMEM((2, 3, 256, 256), BF16),
            dma((7,)), dma((4,)), dma((4,)), dma((4,)), dma((4,)), dma((28,)), dma((28,)),
        ],
        compiler_params=pltpu.CompilerParams(
            collective_id=0, has_side_effects=True, vmem_limit_bytes=32 * 2**20),
        name="h2_product",
    )(near_index, near_count, far_index, vectors, leaf_basis, near_blocks, leaf_couple, leaf_transfer, level_couple, level_transfer)


def solution(mesh):
    dim = P(("gx", "gy"))
    in_specs = (dim, dim, dim, dim, dim, dim, dim, dim, P(None, ("gx", "gy")), P(None, ("gx", "gy")))
    return jax.shard_map(on_device, mesh=mesh, in_specs=in_specs, out_specs=dim, check_vma=False)
```

```python
import jax
import jax.numpy as jnp
from jax import lax
from jax.experimental import pallas as pl
from jax.experimental.pallas import tpu as pltpu
from jax.sharding import PartitionSpec as P

MESH = pl.DeviceIdType.MESH
NODES = 512
OFFSETS = (-3, -2, 2, 3)
NEAR_OFFSETS = (-2, -1, 1, 2)
F32, BF16 = jnp.float32, jnp.bfloat16


def split(x):
    high = x.astype(BF16)
    return high, (x - high.astype(F32)).astype(BF16)


def dot(a, b):
    return jnp.dot(a, b, preferred_element_type=F32)


def dot_t(a, b):
    return lax.dot_general(a, b, (((1,), (1,)), ((), ())), preferred_element_type=F32)


def twice(dot_fn, x, w):
    rows = x.shape[0]
    both = dot_fn(jnp.concatenate(split(x), axis=0), w)
    return both[:rows] + both[rows:]


def packed(x):
    x = x.astype(BF16)
    return jnp.concatenate([x[:16], x[16:]], axis=1)


def where_is(index):
    return (index // 32, lax.rem(index, 32))


def partners(me):
    out = []
    for level in (2, 1, 0):
        members = 2**level
        cluster, member = me // members, lax.rem(me, members)
        first = (0, 4, 12)[level]
        for slot, offset in enumerate(OFFSETS):
            for c in range(members):
                to = (cluster - offset) * members + c
                out.append((level, to, first + slot * members + member, (cluster + offset) * members + c, first + slot * members + c))
    return out


def kernel(
    near_index_hbm, near_count_hbm, far_index_hbm,
    vectors_hbm, basis_hbm, near_hbm, couple_hbm, transfer_hbm, lcouple_hbm, ltransfer_hbm,
    out_ref,
    window, basis, blocks, couple, transfer, lcouple, ltransfer,
    coeffs, doubled, ups, arrived, weights, near_index, near_count, far_index,
    load_sem, vec_send, vec_recv, coef_send, coef_recv, up_send, up_recv,
):
    me = lax.axis_index("gx") * 32 + lax.axis_index("gy")

    def inside(device):
        return jnp.logical_and(device >= 0, device < NODES)

    loads = [
        pltpu.make_async_copy(source, target, load_sem.at[i])
        for i, (source, target) in enumerate((
            (vectors_hbm, window.at[pl.ds(8, 4)]),
            (basis_hbm, basis),
            (transfer_hbm, transfer),
            (ltransfer_hbm, ltransfer),
            (lcouple_hbm, lcouple),
            (couple_hbm, couple),
            (near_hbm, blocks),
            (near_index_hbm, near_index),
            (near_count_hbm, near_count),
            (far_index_hbm, far_index),
        ))
    ]
    for load in loads:
        load.start()

    far = partners(me)
    barrier = pltpu.get_barrier_semaphore()
    greeted = [me + d for d in NEAR_OFFSETS] + [p[1] for p in far]
    expected = jnp.int32(0)
    for device in greeted:
        there = inside(device)
        expected = expected + there.astype(jnp.int32)

        @pl.when(there)
        def _():
            pl.semaphore_signal(barrier, inc=1, device_id=where_is(device), device_id_type=MESH)

    for _, _, _, source, slot in far:
        @pl.when(jnp.logical_not(inside(source)))
        def _():
            arrived[slot] = jnp.zeros((16, 128), BF16)

    pl.semaphore_wait(barrier, expected)

    def vec_copy(i, d):
        return pltpu.make_async_remote_copy(
            src_ref=vectors_hbm, dst_ref=window.at[pl.ds((2 - d) * 4, 4)],
            send_sem=vec_send.at[i], recv_sem=vec_recv.at[3 - i],
            device_id=where_is(me + d), device_id_type=MESH)

    def coef_copy(i, d):
        return pltpu.make_async_remote_copy(
            src_ref=coeffs.at[2], dst_ref=coeffs.at[2 - d],
            send_sem=coef_send.at[i], recv_sem=coef_recv.at[3 - i],
            device_id=where_is(me + d), device_id_type=MESH)

    def up_copy(i):
        level, to, slot, _, _ = far[i]
        return pltpu.make_async_remote_copy(
            src_ref=ups.at[level], dst_ref=arrived.at[slot],
            send_sem=up_send.at[i], recv_sem=up_recv.at[slot],
            device_id=where_is(to), device_id_type=MESH)

    for i, d in enumerate(NEAR_OFFSETS):
        pl.when(inside(me + d))(vec_copy(i, d).start)

    for load in loads[:4]:
        load.wait()
    own = [dot_t(window[8 + t], basis[t]).astype(BF16) for t in range(4)]
    coefficients = jnp.concatenate(own, axis=1)
    coeffs[2] = coefficients
    up0 = dot(coefficients, transfer[...].reshape(256, 64))
    up1 = twice(dot, up0, ltransfer[0, 0])
    up2 = twice(dot, up1, ltransfer[1, 0])
    ups[0] = packed(up0)
    ups[1] = packed(up1)
    ups[2] = packed(up2)
    for i, p in enumerate(far):
        pl.when(inside(p[1]))(up_copy(i).start)
    for i, d in enumerate(NEAR_OFFSETS):
        pl.when(inside(me + d))(coef_copy(i, d).start)

    loads[4].wait()
    transfer_all = transfer[...].reshape(256, 64)
    step = lcouple[0, 0].reshape(256, 64)
    mats = [step.astype(F32)]
    mats.append(dot_t(lcouple[1, 0].reshape(256, 64), ltransfer[0, 0]))
    mats.append(twice(dot_t, dot_t(lcouple[2, 0].reshape(256, 64), ltransfer[1, 0]), ltransfer[0, 0]))
    for level in range(3):
        high, low = split(twice(dot_t, mats[level], transfer_all))
        weights[0, level] = high
        weights[1, level] = low

    lane = lax.broadcasted_iota(jnp.int32, (32, 128), 1)
    left = lane < 64
    left16 = left[:16]

    def level_part(level):
        members = 2**level
        first = (0, 4, 12)[level]
        sums = []
        for slot in range(4):
            total = arrived[first + slot * members].astype(F32)
            for c in range(1, members):
                total = total + arrived[first + slot * members + c].astype(F32)
            sums.append(total)
        parts = []
        for a, b in ((0, 1), (2, 3)):
            top = jnp.where(left16, sums[a], pltpu.roll(sums[b], 64, 1))
            low = jnp.where(left16, pltpu.roll(sums[a], 64, 1), sums[b])
            parts.append(jnp.concatenate([top, low], axis=0))
        high, low = split(jnp.concatenate(parts, axis=1))
        both = dot(jnp.concatenate([high, low], axis=0), weights[0, level])
        return both[:32] + both[32:] + dot(high, weights[1, level])

    def wait_level(level):
        first, count = ((0, 4), (4, 8), (12, 16))[level]
        for i, (_, _, _, source, slot) in enumerate(far):
            if first <= slot_of[i] < first + count:
                pl.when(inside(source))(
                    pltpu.make_async_remote_copy(
                        src_ref=ups.at[level], dst_ref=arrived.at[slot],
                        send_sem=up_send.at[i], recv_sem=up_recv.at[slot],
                        device_id=where_is(source), device_id_type=MESH).wait_recv)

    slot_of = [p[4] for p in far]

    for i, d in enumerate(NEAR_OFFSETS):
        pl.when(inside(me - d))(coef_copy(i, d).wait_recv)

    loads[5].wait()
    loads[9].wait()
    for block in range(5):
        for pair in range(2):
            two = coeffs[block, :, pl.ds(pair * 128, 128)].astype(F32)
            turned = pltpu.roll(two, 64, 1)
            doubled[block * 4 + pair * 2] = jnp.where(left, two, turned).astype(BF16)
            doubled[block * 4 + pair * 2 + 1] = jnp.where(left, turned, two).astype(BF16)
    base = (me - 2) * 4

    def place(leaf):
        return jnp.clip(leaf - base, 0, 19)

    local = []
    for t in range(4):
        cols = []
        for j in range(0, 6, 2):
            first = doubled[place(far_index[t, j])]
            second = doubled[place(far_index[t, j + 1])]
            cols.append(jnp.where(left, first, second))
        local.append(dot(jnp.concatenate(cols, axis=1), couple[t].reshape(384, 64)))
    field = jnp.concatenate(local, axis=1)

    wait_level(0)
    field = field + level_part(0)

    loads[6].wait()
    loads[7].wait()
    loads[8].wait()
    for i, d in enumerate(NEAR_OFFSETS):
        pl.when(inside(me - d))(vec_copy(i, d).wait_recv)
    for t in range(4):
        picked = []
        for j in range(3):
            rows = window[place(near_index[t, j])]
            picked.append(jnp.where(j < near_count[t], rows, jnp.zeros_like(rows)))
        out_ref[t] = dot(jnp.concatenate(picked, axis=1), blocks[t].reshape(768, 256))

    wait_level(1)
    field = field + level_part(1)
    for i, d in enumerate(NEAR_OFFSETS):
        pl.when(inside(me + d))(vec_copy(i, d).wait_send)
        pl.when(inside(me + d))(coef_copy(i, d).wait_send)
    for i, p in enumerate(far):
        pl.when(inside(p[1]))(up_copy(i).wait_send)
    wait_level(2)
    field = (field + level_part(2)).astype(BF16)
    for t in range(4):
        out_ref[t] = out_ref[t] + dot(field[:, t * 64:(t + 1) * 64], basis[t])


def on_device(vectors, leaf_basis, near_blocks, near_index, near_count, leaf_couple, far_index, leaf_transfer, level_couple, level_transfer):
    hbm = pl.BlockSpec(memory_space=pltpu.HBM)
    dma = pltpu.SemaphoreType.DMA
    return pl.pallas_call(
        kernel,
        out_shape=jax.ShapeDtypeStruct((4, 32, 256), F32),
        in_specs=[hbm] * 10,
        out_specs=pl.BlockSpec(memory_space=pltpu.VMEM),
        scratch_shapes=[
            pltpu.VMEM((20, 32, 256), BF16),
            pltpu.VMEM((4, 64, 256), BF16),
            pltpu.VMEM((4, 3, 256, 256), BF16),
            pltpu.VMEM((4, 6, 64, 64), BF16),
            pltpu.VMEM((4, 64, 64), BF16),
            pltpu.VMEM((3, 1, 4, 64, 64), BF16),
            pltpu.VMEM((2, 1, 64, 64), BF16),
            pltpu.VMEM((5, 32, 256), BF16),
            pltpu.VMEM((20, 32, 128), BF16),
            pltpu.VMEM((3, 16, 128), BF16),
            pltpu.VMEM((28, 16, 128), BF16),
            pltpu.VMEM((2, 3, 256, 256), BF16),
            pltpu.SMEM((4, 3), jnp.int32),
            pltpu.SMEM((4,), jnp.int32),
            pltpu.SMEM((4, 6), jnp.int32),
            dma((10,)), dma((4,)), dma((4,)), dma((4,)), dma((4,)), dma((28,)), dma((28,)),
        ],
        compiler_params=pltpu.CompilerParams(
            collective_id=0, has_side_effects=True, vmem_limit_bytes=32 * 2**20),
        name="h2_product",
    )(*(pltpu.with_memory_space_constraint(x, pltpu.HBM) for x in (near_index, near_count, far_index, vectors, jnp.swapaxes(leaf_basis, 1, 2), near_blocks, leaf_couple, leaf_transfer, level_couple, level_transfer)))


def solution(mesh):
    dim = P(("gx", "gy"))
    in_specs = (dim, dim, dim, dim, dim, dim, dim, dim, P(None, ("gx", "gy")), P(None, ("gx", "gy")))
    return jax.shard_map(on_device, mesh=mesh, in_specs=in_specs, out_specs=dim, check_vma=False)
```

```python
import jax
import jax.numpy as jnp
from jax import lax
from jax.experimental import pallas as pl
from jax.experimental.pallas import tpu as pltpu
from jax.sharding import PartitionSpec as P

MESH = pl.DeviceIdType.MESH
NODES = 512
OFFSETS = (-3, -2, 2, 3)
NEAR_OFFSETS = (-2, -1, 1, 2)
F32, BF16 = jnp.float32, jnp.bfloat16


def split(x):
    high = x.astype(BF16)
    return high, (x - high.astype(F32)).astype(BF16)


def dot(a, b):
    return jnp.dot(a, b, preferred_element_type=F32)


def dot_t(a, b):
    return lax.dot_general(a, b, (((1,), (1,)), ((), ())), preferred_element_type=F32)


def twice(dot_fn, x, w):
    rows = x.shape[0]
    both = dot_fn(jnp.concatenate(split(x), axis=0), w)
    return both[:rows] + both[rows:]


def packed(x):
    x = x.astype(BF16)
    return jnp.concatenate([x[:16], x[16:]], axis=1)


def where_is(index):
    return (jnp.right_shift(index, 5), jnp.bitwise_and(index, 31))


FIRST = (0, 4, 12)


def both(a, b):
    return jnp.logical_and(a, b)


def kernel(
    near_index_hbm, near_count_hbm, far_index_hbm,
    vectors_hbm, basis_hbm, near_hbm, couple_hbm, transfer_hbm, lcouple_hbm, ltransfer_hbm,
    out_ref,
    window, basis, blocks, couple, transfer, lcouple, ltransfer,
    coeffs, doubled, ups, arrived, weights, near_index, near_count, far_index,
    load_sem, vec_send, vec_recv, coef_send, coef_recv, up_send, up_recv, known,
):
    me = lax.axis_index("gx") * 32 + lax.axis_index("gy")

    def inside(device):
        return jnp.logical_and(device >= 0, device < NODES)

    loads = [
        pltpu.make_async_copy(source, target, load_sem.at[i])
        for i, (source, target) in enumerate((
            (vectors_hbm, window.at[pl.ds(8, 4)]),
            (basis_hbm, basis),
            (transfer_hbm, transfer),
            (ltransfer_hbm, ltransfer),
            (lcouple_hbm, lcouple),
            (couple_hbm, couple),
            (near_hbm, blocks),
            (near_index_hbm, near_index),
            (near_count_hbm, near_count),
            (far_index_hbm, far_index),
        ))
    ]
    for load in loads:
        load.start()

    barrier = pltpu.get_barrier_semaphore()

    def tell(semaphore, distances):
        count = jnp.int32(0)
        for d in distances:
            there = inside(me + d)
            count = count + there.astype(jnp.int32)

            @pl.when(there)
            def _():
                pl.semaphore_signal(semaphore, inc=1, device_id=where_is(me + d), device_id_type=MESH)

        return count

    beside = tell(barrier, (-4, 4, -3, 3, -2, 2, -1, 1))

    for level in range(3):
        members = 2**level
        cluster = jnp.right_shift(me, level)
        for slot, offset in enumerate(OFFSETS):
            source = cluster + offset

            @pl.when(jnp.logical_or(source < 0, source >= NODES // members))
            def _():
                for c in range(members):
                    arrived[FIRST[level] + slot * members + c] = jnp.zeros((16, 128), BF16)

    def vec_copy(i, d):
        return pltpu.make_async_remote_copy(
            src_ref=vectors_hbm, dst_ref=window.at[pl.ds((2 - d) * 4, 4)],
            send_sem=vec_send.at[i], recv_sem=vec_recv.at[3 - i],
            device_id=where_is(me + d), device_id_type=MESH)

    def coef_copy(i, d):
        return pltpu.make_async_remote_copy(
            src_ref=coeffs.at[2], dst_ref=coeffs.at[2 - d],
            send_sem=coef_send.at[i], recv_sem=coef_recv.at[3 - i],
            device_id=where_is(me + d), device_id_type=MESH)

    def up_copy(level, slot, c):
        members = 2**level
        first = FIRST[level] + slot * members
        return pltpu.make_async_remote_copy(
            src_ref=ups.at[level], dst_ref=arrived.at[first + jnp.bitwise_and(me, members - 1)],
            send_sem=up_send.at[first + c], recv_sem=up_recv.at[first + jnp.bitwise_and(me, members - 1)],
            device_id=where_is((jnp.right_shift(me, level) - OFFSETS[slot]) * members + c), device_id_type=MESH)

    def arrival(level, slot, c):
        place = FIRST[level] + slot * 2**level + c
        return pltpu.make_async_remote_copy(
            src_ref=ups.at[level], dst_ref=arrived.at[place],
            send_sem=up_send.at[place], recv_sem=up_recv.at[place],
            device_id=where_is(jnp.bitwise_and(me + 1, NODES - 1)), device_id_type=MESH)

    def goes(level, slot):
        to = jnp.right_shift(me, level) - OFFSETS[slot]
        return both(to >= 0, to < NODES // 2**level)

    def comes(level, slot):
        source = jnp.right_shift(me, level) + OFFSETS[slot]
        return both(source >= 0, source < NODES // 2**level)

    def send_up(level, slot):
        @pl.when(goes(level, slot))
        def _():
            for c in range(2**level):
                up_copy(level, slot, c).start()

    for load in loads[:4]:
        load.wait()
    own = [dot_t(window[8 + t], basis[t]).astype(BF16) for t in range(4)]
    coefficients = jnp.concatenate(own, axis=1)
    coeffs[2] = coefficients
    up0 = dot(coefficients, transfer[...].reshape(256, 64))
    up1 = twice(dot, up0, ltransfer[0, 0])
    up2 = twice(dot, up1, ltransfer[1, 0])
    ups[0] = packed(up0)
    ups[1] = packed(up1)
    ups[2] = packed(up2)

    pl.semaphore_wait(barrier, beside)
    relayed = tell(known.at[0], (-4, 4))
    for i, d in enumerate(NEAR_OFFSETS):
        @pl.when(inside(me + d))
        def _():
            coef_copy(i, d).start()
            vec_copy(i, d).start()
    for slot in range(4):
        send_up(0, slot)
    pl.semaphore_wait(known.at[0], relayed)
    relayed = tell(known.at[1], (-8, 8))
    for slot in range(4):
        send_up(1, slot)
    pl.semaphore_wait(known.at[1], relayed)
    for slot in (0, 3, 1, 2):
        send_up(2, slot)

    loads[4].wait()
    transfer_all = transfer[...].reshape(256, 64)
    step = lcouple[0, 0].reshape(256, 64)
    mats = [step.astype(F32)]
    mats.append(dot_t(lcouple[1, 0].reshape(256, 64), ltransfer[0, 0]))
    mats.append(twice(dot_t, dot_t(lcouple[2, 0].reshape(256, 64), ltransfer[1, 0]), ltransfer[0, 0]))
    for level in range(3):
        high, low = split(twice(dot_t, mats[level], transfer_all))
        weights[0, level] = high
        weights[1, level] = low

    lane = lax.broadcasted_iota(jnp.int32, (32, 128), 1)
    left = lane < 64
    left16 = left[:16]

    def level_part(level):
        members = 2**level
        first = (0, 4, 12)[level]
        sums = []
        for slot in range(4):
            total = arrived[first + slot * members].astype(F32)
            for c in range(1, members):
                total = total + arrived[first + slot * members + c].astype(F32)
            sums.append(total)
        parts = []
        for a, b in ((0, 1), (2, 3)):
            top = jnp.where(left16, sums[a], pltpu.roll(sums[b], 64, 1))
            low = jnp.where(left16, pltpu.roll(sums[a], 64, 1), sums[b])
            parts.append(jnp.concatenate([top, low], axis=0))
        high, low = split(jnp.concatenate(parts, axis=1))
        both = dot(jnp.concatenate([high, low], axis=0), weights[0, level])
        return both[:32] + both[32:] + dot(high, weights[1, level])

    def wait_level(level):
        for slot in range(4):
            @pl.when(comes(level, slot))
            def _():
                for c in range(2**level):
                    arrival(level, slot, c).wait_recv()

    for i, d in enumerate(NEAR_OFFSETS):
        pl.when(inside(me - d))(coef_copy(i, d).wait_recv)

    loads[5].wait()
    loads[9].wait()
    for block in range(5):
        for pair in range(2):
            two = coeffs[block, :, pl.ds(pair * 128, 128)].astype(F32)
            turned = pltpu.roll(two, 64, 1)
            doubled[block * 4 + pair * 2] = jnp.where(left, two, turned).astype(BF16)
            doubled[block * 4 + pair * 2 + 1] = jnp.where(left, turned, two).astype(BF16)
    base = (me - 2) * 4

    def place(leaf):
        return jnp.clip(leaf - base, 0, 19)

    local = []
    for t in range(4):
        cols = []
        for j in range(0, 6, 2):
            first = doubled[place(far_index[t, j])]
            second = doubled[place(far_index[t, j + 1])]
            cols.append(jnp.where(left, first, second))
        local.append(dot(jnp.concatenate(cols, axis=1), couple[t].reshape(384, 64)))
    field = jnp.concatenate(local, axis=1)

    wait_level(0)
    field = field + level_part(0)

    loads[6].wait()
    loads[7].wait()
    loads[8].wait()
    for i, d in enumerate(NEAR_OFFSETS):
        pl.when(inside(me - d))(vec_copy(i, d).wait_recv)
    for t in range(4):
        picked = []
        for j in range(3):
            rows = window[place(near_index[t, j])]
            picked.append(jnp.where(j < near_count[t], rows, jnp.zeros_like(rows)))
        out_ref[t] = dot(jnp.concatenate(picked, axis=1), blocks[t].reshape(768, 256))

    wait_level(1)
    field = field + level_part(1)
    wait_level(2)
    field = (field + level_part(2)).astype(BF16)
    for t in range(4):
        out_ref[t] = out_ref[t] + dot(field[:, t * 64:(t + 1) * 64], basis[t])

    for i, d in enumerate(NEAR_OFFSETS):
        @pl.when(inside(me + d))
        def _():
            vec_copy(i, d).wait_send()
            coef_copy(i, d).wait_send()
    for level in range(3):
        for slot in range(4):
            @pl.when(goes(level, slot))
            def _():
                for c in range(2**level):
                    up_copy(level, slot, c).wait_send()


def on_device(vectors, leaf_basis, near_blocks, near_index, near_count, leaf_couple, far_index, leaf_transfer, level_couple, level_transfer):
    hbm = pl.BlockSpec(memory_space=pltpu.HBM)
    dma = pltpu.SemaphoreType.DMA
    return pl.pallas_call(
        kernel,
        out_shape=jax.ShapeDtypeStruct((4, 32, 256), F32),
        in_specs=[hbm] * 10,
        out_specs=pl.BlockSpec(memory_space=pltpu.VMEM),
        scratch_shapes=[
            pltpu.VMEM((20, 32, 256), BF16),
            pltpu.VMEM((4, 64, 256), BF16),
            pltpu.VMEM((4, 3, 256, 256), BF16),
            pltpu.VMEM((4, 6, 64, 64), BF16),
            pltpu.VMEM((4, 64, 64), BF16),
            pltpu.VMEM((3, 1, 4, 64, 64), BF16),
            pltpu.VMEM((2, 1, 64, 64), BF16),
            pltpu.VMEM((5, 32, 256), BF16),
            pltpu.VMEM((20, 32, 128), BF16),
            pltpu.VMEM((3, 16, 128), BF16),
            pltpu.VMEM((28, 16, 128), BF16),
            pltpu.VMEM((2, 3, 256, 256), BF16),
            pltpu.SMEM((4, 3), jnp.int32),
            pltpu.SMEM((4,), jnp.int32),
            pltpu.SMEM((4, 6), jnp.int32),
            dma((10,)), dma((4,)), dma((4,)), dma((4,)), dma((4,)), dma((28,)), dma((28,)), pltpu.SemaphoreType.REGULAR((2,)),
        ],
        compiler_params=pltpu.CompilerParams(
            collective_id=0, has_side_effects=True, vmem_limit_bytes=32 * 2**20),
        name="h2_product",
    )(*(pltpu.with_memory_space_constraint(x, pltpu.HBM) for x in (near_index, near_count, far_index, vectors, jnp.swapaxes(leaf_basis, 1, 2), near_blocks, leaf_couple, leaf_transfer, level_couple, level_transfer)))


def solution(mesh):
    dim = P(("gx", "gy"))
    in_specs = (dim, dim, dim, dim, dim, dim, dim, dim, P(None, ("gx", "gy")), P(None, ("gx", "gy")))
    return jax.shard_map(on_device, mesh=mesh, in_specs=in_specs, out_specs=dim, check_vma=False)
```

```python
import jax
import jax.numpy as jnp
from jax import lax
from jax.experimental import pallas as pl
from jax.experimental.pallas import tpu as pltpu
from jax.sharding import PartitionSpec as P

MESH = pl.DeviceIdType.MESH
NODES = 512
OFFSETS = (-3, -2, 2, 3)
NEAR_OFFSETS = (-2, -1, 1, 2)
F32, BF16 = jnp.float32, jnp.bfloat16


def split(x):
    high = x.astype(BF16)
    return high, (x - high.astype(F32)).astype(BF16)


def dot(a, b):
    return jnp.dot(a, b, preferred_element_type=F32)


def dot_t(a, b):
    return lax.dot_general(a, b, (((1,), (1,)), ((), ())), preferred_element_type=F32)


def twice(dot_fn, x, w):
    rows = x.shape[0]
    both = dot_fn(jnp.concatenate(split(x), axis=0), w)
    return both[:rows] + both[rows:]


def packed(x):
    x = x.astype(BF16)
    return jnp.concatenate([x[:16], x[16:]], axis=1)


def where_is(index):
    return (jnp.right_shift(index, 5), jnp.bitwise_and(index, 31))


FIRST = (0, 4, 8)
CHIPS = (1, 1, 2)


def both(a, b):
    return jnp.logical_and(a, b)


def kernel(
    near_index_hbm, near_count_hbm, far_index_hbm,
    vectors_hbm, basis_hbm, near_hbm, couple_hbm, transfer_hbm, lcouple_hbm, ltransfer_hbm,
    out_ref,
    window, basis, blocks, couple, transfer, lcouple, ltransfer,
    coeffs, doubled, ups, arrived, weights, halves, near_index, near_count, far_index,
    load_sem, vec_send, vec_recv, coef_send, coef_recv, up_send, up_recv, swap_sem, known,
):
    me = lax.axis_index("gx") * 32 + lax.axis_index("gy")

    def inside(device):
        return jnp.logical_and(device >= 0, device < NODES)

    loads = [
        pltpu.make_async_copy(source, target, load_sem.at[i])
        for i, (source, target) in enumerate((
            (vectors_hbm, window.at[pl.ds(8, 4)]),
            (basis_hbm, basis),
            (transfer_hbm, transfer),
            (ltransfer_hbm, ltransfer),
            (lcouple_hbm, lcouple),
            (couple_hbm, couple),
            (near_hbm, blocks),
            (near_index_hbm, near_index),
            (near_count_hbm, near_count),
            (far_index_hbm, far_index),
        ))
    ]
    for load in loads:
        load.start()

    barrier = pltpu.get_barrier_semaphore()

    def tell(semaphore, distances):
        count = jnp.int32(0)
        for d in distances:
            there = inside(me + d)
            count = count + there.astype(jnp.int32)

            @pl.when(there)
            def _():
                pl.semaphore_signal(semaphore, inc=1, device_id=where_is(me + d), device_id_type=MESH)

        return count

    beside = tell(barrier, (-8, 8, -6, 6, -4, 4, -3, 3, -2, 2, -1, 1))

    for level in range(3):
        members = 2**level
        cluster = jnp.right_shift(me, level)
        for slot, offset in enumerate(OFFSETS):
            source = cluster + offset

            @pl.when(jnp.logical_or(source < 0, source >= NODES // members))
            def _():
                for c in range(CHIPS[level]):
                    arrived[FIRST[level] + slot * CHIPS[level] + c] = jnp.zeros((16, 128), BF16)

    def vec_copy(i, d):
        return pltpu.make_async_remote_copy(
            src_ref=vectors_hbm, dst_ref=window.at[pl.ds((2 - d) * 4, 4)],
            send_sem=vec_send.at[i], recv_sem=vec_recv.at[3 - i],
            device_id=where_is(me + d), device_id_type=MESH)

    def coef_copy(i, d):
        return pltpu.make_async_remote_copy(
            src_ref=coeffs.at[2], dst_ref=coeffs.at[2 - d],
            send_sem=coef_send.at[i], recv_sem=coef_recv.at[3 - i],
            device_id=where_is(me + d), device_id_type=MESH)

    core, chip = jnp.bitwise_and(me, 1), jnp.bitwise_and(jnp.right_shift(me, 1), 1)

    def up_copy(level, slot, c):
        first = FIRST[level] + slot * CHIPS[level]
        if level == 2:
            to, mine = (jnp.right_shift(me, 2) - OFFSETS[slot]) * 4 + 2 * c + core, first + chip
        else:
            to, mine = me - OFFSETS[slot] * 2**level, first
        return pltpu.make_async_remote_copy(
            src_ref=ups.at[level], dst_ref=arrived.at[mine],
            send_sem=up_send.at[first + c], recv_sem=up_recv.at[mine],
            device_id=where_is(to), device_id_type=MESH)

    def arrival(level, slot, c):
        place = FIRST[level] + slot * CHIPS[level] + c
        return pltpu.make_async_remote_copy(
            src_ref=ups.at[level], dst_ref=arrived.at[place],
            send_sem=up_send.at[place], recv_sem=up_recv.at[place],
            device_id=where_is(jnp.bitwise_and(me + 1, NODES - 1)), device_id_type=MESH)

    swap = pltpu.make_async_remote_copy(
        src_ref=halves.at[0], dst_ref=halves.at[1], send_sem=swap_sem.at[0], recv_sem=swap_sem.at[1],
        device_id=where_is(jnp.bitwise_xor(me, 1)), device_id_type=MESH)

    def goes(level, slot):
        to = jnp.right_shift(me, level) - OFFSETS[slot]
        return both(to >= 0, to < NODES // 2**level)

    def comes(level, slot):
        source = jnp.right_shift(me, level) + OFFSETS[slot]
        return both(source >= 0, source < NODES // 2**level)

    def send_up(level, slot):
        @pl.when(goes(level, slot))
        def _():
            for c in range(CHIPS[level]):
                up_copy(level, slot, c).start()

    for load in loads[:4]:
        load.wait()
    own = [dot_t(window[8 + t], basis[t]).astype(BF16) for t in range(4)]
    coefficients = jnp.concatenate(own, axis=1)
    coeffs[2] = coefficients
    up0 = dot(coefficients, transfer[...].reshape(256, 64))
    up1 = twice(dot, up0, ltransfer[0, 0])
    ups[0] = packed(up0)
    half = jnp.concatenate([up1[:16], up1[16:]], axis=1)
    high, low = split(half)
    halves[0, 0] = high
    halves[0, 1] = low

    pl.semaphore_wait(barrier, beside)
    relayed = tell(known.at[0], (-8, 8))
    swap.start()
    for i, d in enumerate(NEAR_OFFSETS):
        @pl.when(inside(me + d))
        def _():
            coef_copy(i, d).start()
            vec_copy(i, d).start()
    for slot in range(4):
        send_up(0, slot)
    swap.wait_recv()
    half = half + (halves[1, 0].astype(F32) + halves[1, 1].astype(F32))
    ups[1] = half.astype(BF16)
    turned = pltpu.roll(half, 64, 1)
    pair = jnp.concatenate([half, turned], axis=0)[:, :64]
    ups[2] = packed(twice(dot, pair, ltransfer[1, 0]))
    for slot in range(4):
        send_up(1, slot)
    pl.semaphore_wait(known.at[0], relayed)
    for slot in (0, 3, 1, 2):
        send_up(2, slot)

    loads[4].wait()
    transfer_all = transfer[...].reshape(256, 64)
    step = lcouple[0, 0].reshape(256, 64)
    mats = [step.astype(F32)]
    mats.append(dot_t(lcouple[1, 0].reshape(256, 64), ltransfer[0, 0]))
    mats.append(twice(dot_t, dot_t(lcouple[2, 0].reshape(256, 64), ltransfer[1, 0]), ltransfer[0, 0]))
    for level in range(3):
        high, low = split(twice(dot_t, mats[level], transfer_all))
        weights[0, level] = high
        weights[1, level] = low

    lane = lax.broadcasted_iota(jnp.int32, (32, 128), 1)
    left = lane < 64
    left16 = left[:16]

    def level_part(level):
        sums = []
        for slot in range(4):
            place = FIRST[level] + slot * CHIPS[level]
            total = arrived[place].astype(F32)
            for c in range(1, CHIPS[level]):
                total = total + arrived[place + c].astype(F32)
            sums.append(total)
        parts = []
        for a, b in ((0, 1), (2, 3)):
            top = jnp.where(left16, sums[a], pltpu.roll(sums[b], 64, 1))
            low = jnp.where(left16, pltpu.roll(sums[a], 64, 1), sums[b])
            parts.append(jnp.concatenate([top, low], axis=0))
        high, low = split(jnp.concatenate(parts, axis=1))
        both = dot(jnp.concatenate([high, low], axis=0), weights[0, level])
        return both[:32] + both[32:] + dot(high, weights[1, level])

    def wait_level(level):
        for slot in range(4):
            @pl.when(comes(level, slot))
            def _():
                for c in range(CHIPS[level]):
                    arrival(level, slot, c).wait_recv()

    for i, d in enumerate(NEAR_OFFSETS):
        pl.when(inside(me - d))(coef_copy(i, d).wait_recv)

    loads[5].wait()
    loads[9].wait()
    for block in range(5):
        for pair in range(2):
            two = coeffs[block, :, pl.ds(pair * 128, 128)].astype(F32)
            turned = pltpu.roll(two, 64, 1)
            doubled[block * 4 + pair * 2] = jnp.where(left, two, turned).astype(BF16)
            doubled[block * 4 + pair * 2 + 1] = jnp.where(left, turned, two).astype(BF16)
    base = (me - 2) * 4

    def place(leaf):
        return jnp.clip(leaf - base, 0, 19)

    local = []
    for t in range(4):
        cols = []
        for j in range(0, 6, 2):
            first = doubled[place(far_index[t, j])]
            second = doubled[place(far_index[t, j + 1])]
            cols.append(jnp.where(left, first, second))
        local.append(dot(jnp.concatenate(cols, axis=1), couple[t].reshape(384, 64)))
    field = jnp.concatenate(local, axis=1)

    wait_level(0)
    field = field + level_part(0)

    loads[6].wait()
    loads[7].wait()
    loads[8].wait()
    for i, d in enumerate(NEAR_OFFSETS):
        pl.when(inside(me - d))(vec_copy(i, d).wait_recv)
    for t in range(4):
        picked = []
        for j in range(3):
            rows = window[place(near_index[t, j])]
            picked.append(jnp.where(j < near_count[t], rows, jnp.zeros_like(rows)))
        out_ref[t] = dot(jnp.concatenate(picked, axis=1), blocks[t].reshape(768, 256))

    wait_level(1)
    field = field + level_part(1)
    wait_level(2)
    field = (field + level_part(2)).astype(BF16)
    for t in range(4):
        out_ref[t] = out_ref[t] + dot(field[:, t * 64:(t + 1) * 64], basis[t])

    swap.wait_send()
    for i, d in enumerate(NEAR_OFFSETS):
        @pl.when(inside(me + d))
        def _():
            vec_copy(i, d).wait_send()
            coef_copy(i, d).wait_send()
    for level in range(3):
        for slot in range(4):
            @pl.when(goes(level, slot))
            def _():
                for c in range(CHIPS[level]):
                    up_copy(level, slot, c).wait_send()


def on_device(vectors, leaf_basis, near_blocks, near_index, near_count, leaf_couple, far_index, leaf_transfer, level_couple, level_transfer):
    hbm = pl.BlockSpec(memory_space=pltpu.HBM)
    dma = pltpu.SemaphoreType.DMA
    return pl.pallas_call(
        kernel,
        out_shape=jax.ShapeDtypeStruct((4, 32, 256), F32),
        in_specs=[hbm] * 10,
        out_specs=pl.BlockSpec(memory_space=pltpu.VMEM),
        scratch_shapes=[
            pltpu.VMEM((20, 32, 256), BF16),
            pltpu.VMEM((4, 64, 256), BF16),
            pltpu.VMEM((4, 3, 256, 256), BF16),
            pltpu.VMEM((4, 6, 64, 64), BF16),
            pltpu.VMEM((4, 64, 64), BF16),
            pltpu.VMEM((3, 1, 4, 64, 64), BF16),
            pltpu.VMEM((2, 1, 64, 64), BF16),
            pltpu.VMEM((5, 32, 256), BF16),
            pltpu.VMEM((20, 32, 128), BF16),
            pltpu.VMEM((3, 16, 128), BF16),
            pltpu.VMEM((16, 16, 128), BF16),
            pltpu.VMEM((2, 3, 256, 256), BF16),
            pltpu.VMEM((2, 2, 16, 128), BF16),
            pltpu.SMEM((4, 3), jnp.int32),
            pltpu.SMEM((4,), jnp.int32),
            pltpu.SMEM((4, 6), jnp.int32),
            dma((10,)), dma((4,)), dma((4,)), dma((4,)), dma((4,)), dma((16,)), dma((16,)), dma((2,)), pltpu.SemaphoreType.REGULAR((1,)),
        ],
        compiler_params=pltpu.CompilerParams(
            collective_id=0, has_side_effects=True, vmem_limit_bytes=32 * 2**20),
        name="h2_product",
    )(*(pltpu.with_memory_space_constraint(x, pltpu.HBM) for x in (near_index, near_count, far_index, vectors, jnp.swapaxes(leaf_basis, 1, 2), near_blocks, leaf_couple, leaf_transfer, level_couple, level_transfer)))


def solution(mesh):
    dim = P(("gx", "gy"))
    in_specs = (dim, dim, dim, dim, dim, dim, dim, dim, P(None, ("gx", "gy")), P(None, ("gx", "gy")))
    return jax.shard_map(on_device, mesh=mesh, in_specs=in_specs, out_specs=dim, check_vma=False)
```

```python
import jax
import jax.numpy as jnp
from jax import lax
from jax.experimental import pallas as pl
from jax.experimental.pallas import tpu as pltpu
from jax.sharding import PartitionSpec as P

MESH = pl.DeviceIdType.MESH
NODES = 512
OFFSETS = (-3, -2, 2, 3)
NEAR_OFFSETS = (-2, -1, 1, 2)
F32, BF16 = jnp.float32, jnp.bfloat16


def split(x):
    high = x.astype(BF16)
    return high, (x - high.astype(F32)).astype(BF16)


def dot(a, b):
    return jnp.dot(a, b, preferred_element_type=F32)


def dot_t(a, b):
    return lax.dot_general(a, b, (((1,), (1,)), ((), ())), preferred_element_type=F32)


def twice(dot_fn, x, w):
    rows = x.shape[0]
    both = dot_fn(jnp.concatenate(split(x), axis=0), w)
    return both[:rows] + both[rows:]


def packed(x):
    x = x.astype(BF16)
    return jnp.concatenate([x[:16], x[16:]], axis=1)


def where_is(index):
    return (jnp.right_shift(index, 5), jnp.bitwise_and(index, 31))


FIRST = (0, 4, 8)
CHIPS = (1, 1, 2)


def both(a, b):
    return jnp.logical_and(a, b)


def kernel(
    near_index_hbm, near_count_hbm, far_index_hbm,
    vectors_hbm, basis_hbm, near_hbm, couple_hbm, transfer_hbm, lcouple_hbm, ltransfer_hbm,
    out_ref,
    window, basis, blocks, couple, transfer, lcouple, ltransfer,
    coeffs, doubled, ups, arrived, weights, halves, near_index, near_count, far_index,
    load_sem, vec_send, vec_recv, coef_send, coef_recv, up_send, up_recv, swap_sem, known,
):
    me = lax.axis_index("gx") * 32 + lax.axis_index("gy")

    def inside(device):
        return jnp.logical_and(device >= 0, device < NODES)

    loads = [
        pltpu.make_async_copy(source, target, load_sem.at[i])
        for i, (source, target) in enumerate((
            (vectors_hbm, window.at[pl.ds(8, 4)]),
            (basis_hbm, basis),
            (transfer_hbm, transfer),
            (ltransfer_hbm, ltransfer),
            (lcouple_hbm, lcouple),
            (couple_hbm, couple),
            (near_hbm, blocks),
            (near_index_hbm, near_index),
            (near_count_hbm, near_count),
            (far_index_hbm, far_index),
        ))
    ]
    for load in loads[:4]:
        load.start()

    barrier = pltpu.get_barrier_semaphore()

    def tell(semaphore, distances):
        count = jnp.int32(0)
        for d in distances:
            there = inside(me + d)
            count = count + there.astype(jnp.int32)

            @pl.when(there)
            def _():
                pl.semaphore_signal(semaphore, inc=1, device_id=where_is(me + d), device_id_type=MESH)

        return count

    beside = tell(barrier, (-8, 8, -6, 6, -4, 4, -3, 3, -2, 2, -1, 1))

    for level in range(3):
        members = 2**level
        cluster = jnp.right_shift(me, level)
        for slot, offset in enumerate(OFFSETS):
            source = cluster + offset

            @pl.when(jnp.logical_or(source < 0, source >= NODES // members))
            def _():
                for c in range(CHIPS[level]):
                    arrived[FIRST[level] + slot * CHIPS[level] + c] = jnp.zeros((16, 128), BF16)

    side = 2 * jnp.bitwise_and(me, 1) - 1

    def vec_copy(role):
        to = (me + side, me - 2 * side, me - side, me - side)[role]
        block = (2 - side, 2 + 2 * side, 2 + side, 2 + 2 * side)[role]
        mine = 2 + side if role == 3 else 2
        return pltpu.make_async_remote_copy(
            src_ref=window.at[pl.ds(mine * 4, 4)], dst_ref=window.at[pl.ds(block * 4, 4)],
            send_sem=vec_send.at[role], recv_sem=vec_recv.at[role],
            device_id=where_is(to), device_id_type=MESH)

    vec_goes = [inside(me + side), inside(me - 2 * side), inside(me - side), inside(me + side)]
    vec_comes = [inside(me + side), inside(me + 2 * side), inside(me - side), inside(me - 2 * side)]

    def coef_copy(i, d):
        return pltpu.make_async_remote_copy(
            src_ref=coeffs.at[2], dst_ref=coeffs.at[2 - d],
            send_sem=coef_send.at[i], recv_sem=coef_recv.at[3 - i],
            device_id=where_is(me + d), device_id_type=MESH)

    core, chip = jnp.bitwise_and(me, 1), jnp.bitwise_and(jnp.right_shift(me, 1), 1)

    def up_copy(level, slot, c):
        first = FIRST[level] + slot * CHIPS[level]
        if level == 2:
            to, mine = (jnp.right_shift(me, 2) - OFFSETS[slot]) * 4 + 2 * c + core, first + chip
        else:
            to, mine = me - OFFSETS[slot] * 2**level, first
        return pltpu.make_async_remote_copy(
            src_ref=ups.at[level], dst_ref=arrived.at[mine],
            send_sem=up_send.at[first + c], recv_sem=up_recv.at[mine],
            device_id=where_is(to), device_id_type=MESH)

    def arrival(level, slot, c):
        place = FIRST[level] + slot * CHIPS[level] + c
        return pltpu.make_async_remote_copy(
            src_ref=ups.at[level], dst_ref=arrived.at[place],
            send_sem=up_send.at[place], recv_sem=up_recv.at[place],
            device_id=where_is(jnp.bitwise_and(me + 1, NODES - 1)), device_id_type=MESH)

    swap = pltpu.make_async_remote_copy(
        src_ref=halves.at[0], dst_ref=halves.at[1], send_sem=swap_sem.at[0], recv_sem=swap_sem.at[1],
        device_id=where_is(jnp.bitwise_xor(me, 1)), device_id_type=MESH)

    def goes(level, slot):
        to = jnp.right_shift(me, level) - OFFSETS[slot]
        return both(to >= 0, to < NODES // 2**level)

    def comes(level, slot):
        source = jnp.right_shift(me, level) + OFFSETS[slot]
        return both(source >= 0, source < NODES // 2**level)

    def send_up(level, slot):
        @pl.when(goes(level, slot))
        def _():
            for c in range(CHIPS[level]):
                up_copy(level, slot, c).start()

    for load in loads[:4]:
        load.wait()
    for load in loads[4:]:
        load.start()
    own = [dot_t(window[8 + t], basis[t]).astype(BF16) for t in range(4)]
    coefficients = jnp.concatenate(own, axis=1)
    coeffs[2] = coefficients
    up0 = dot(coefficients, transfer[...].reshape(256, 64))
    up1 = twice(dot, up0, ltransfer[0, 0])
    ups[0] = packed(up0)
    half = jnp.concatenate([up1[:16], up1[16:]], axis=1)
    high, low = split(half)
    halves[0, 0] = high
    halves[0, 1] = low

    pl.semaphore_wait(barrier, beside)
    below = tell(known.at[1], (-8,))
    above = tell(known.at[0], (8,))
    swap.start()
    for i, d in enumerate(NEAR_OFFSETS):
        @pl.when(inside(me + d))
        def _():
            coef_copy(i, d).start()
    for slot in range(4):
        send_up(0, slot)
    for role in range(3):
        pl.when(vec_goes[role])(vec_copy(role).start)
    swap.wait_recv()
    half = half + (halves[1, 0].astype(F32) + halves[1, 1].astype(F32))
    ups[1] = half.astype(BF16)
    turned = pltpu.roll(half, 64, 1)
    pair = jnp.concatenate([half, turned], axis=0)[:, :64]
    ups[2] = packed(twice(dot, pair, ltransfer[1, 0]))
    for slot in range(4):
        send_up(1, slot)

    def send_two_off(slot, c, close):
        reached = (c <= chip) if slot == 1 else (c >= chip)
        if c == slot - 1:
            if not close:
                return
            reached = True
        elif not close:
            reached = jnp.logical_not(reached)
        pl.when(both(goes(2, slot), reached))(up_copy(2, slot, c).start)

    def to_above():
        @pl.when(above > 0)
        def _():
            pl.semaphore_wait(known.at[1], above)

        send_up(2, 0)
        send_two_off(1, 1, False)

    for slot in (1, 2):
        for c in range(2):
            send_two_off(slot, c, True)
    rising = jnp.bitwise_and(jnp.right_shift(me, 2), 7) < 4
    pl.when(rising)(to_above)

    @pl.when(below > 0)
    def _():
        pl.semaphore_wait(known.at[0], below)

    send_up(2, 3)
    send_two_off(2, 0, False)
    pl.when(jnp.logical_not(rising))(to_above)

    loads[4].wait()
    transfer_all = transfer[...].reshape(256, 64)
    step = lcouple[0, 0].reshape(256, 64)
    mats = [step.astype(F32)]
    mats.append(dot_t(lcouple[1, 0].reshape(256, 64), ltransfer[0, 0]))
    mats.append(twice(dot_t, dot_t(lcouple[2, 0].reshape(256, 64), ltransfer[1, 0]), ltransfer[0, 0]))
    for level in range(3):
        high, low = split(twice(dot_t, mats[level], transfer_all))
        weights[0, level] = high
        weights[1, level] = low

    lane = lax.broadcasted_iota(jnp.int32, (32, 128), 1)
    left = lane < 64
    left16 = left[:16]

    def level_part(level):
        sums = []
        for slot in range(4):
            place = FIRST[level] + slot * CHIPS[level]
            total = arrived[place].astype(F32)
            for c in range(1, CHIPS[level]):
                total = total + arrived[place + c].astype(F32)
            sums.append(total)
        parts = []
        for a, b in ((0, 1), (2, 3)):
            top = jnp.where(left16, sums[a], pltpu.roll(sums[b], 64, 1))
            low = jnp.where(left16, pltpu.roll(sums[a], 64, 1), sums[b])
            parts.append(jnp.concatenate([top, low], axis=0))
        high, low = split(jnp.concatenate(parts, axis=1))
        both = dot(jnp.concatenate([high, low], axis=0), weights[0, level])
        return both[:32] + both[32:] + dot(high, weights[1, level])

    def wait_level(level):
        for slot in range(4):
            @pl.when(comes(level, slot))
            def _():
                for c in range(CHIPS[level]):
                    arrival(level, slot, c).wait_recv()

    @pl.when(vec_comes[0])
    def _():
        vec_copy(0).wait_recv()
        vec_copy(3).start()

    for i, d in enumerate(NEAR_OFFSETS):
        pl.when(inside(me - d))(coef_copy(i, d).wait_recv)

    loads[5].wait()
    loads[9].wait()
    for block in range(5):
        for pair in range(2):
            two = coeffs[block, :, pl.ds(pair * 128, 128)].astype(F32)
            turned = pltpu.roll(two, 64, 1)
            doubled[block * 4 + pair * 2] = jnp.where(left, two, turned).astype(BF16)
            doubled[block * 4 + pair * 2 + 1] = jnp.where(left, turned, two).astype(BF16)
    base = (me - 2) * 4

    def place(leaf):
        return jnp.clip(leaf - base, 0, 19)

    local = []
    for t in range(4):
        cols = []
        for j in range(0, 6, 2):
            first = doubled[place(far_index[t, j])]
            second = doubled[place(far_index[t, j + 1])]
            cols.append(jnp.where(left, first, second))
        local.append(dot(jnp.concatenate(cols, axis=1), couple[t].reshape(384, 64)))
    field = jnp.concatenate(local, axis=1)

    wait_level(0)
    field = field + level_part(0)

    loads[6].wait()
    loads[7].wait()
    loads[8].wait()
    for role in range(1, 4):
        pl.when(vec_comes[role])(vec_copy(role).wait_recv)
    for t in range(4):
        picked = []
        for j in range(3):
            rows = window[place(near_index[t, j])]
            picked.append(jnp.where(j < near_count[t], rows, jnp.zeros_like(rows)))
        out_ref[t] = dot(jnp.concatenate(picked, axis=1), blocks[t].reshape(768, 256))

    wait_level(1)
    field = field + level_part(1)
    wait_level(2)
    field = (field + level_part(2)).astype(BF16)
    for t in range(4):
        out_ref[t] = out_ref[t] + dot(field[:, t * 64:(t + 1) * 64], basis[t])

    swap.wait_send()
    for role in range(4):
        pl.when(vec_goes[role])(vec_copy(role).wait_send)
    for i, d in enumerate(NEAR_OFFSETS):
        @pl.when(inside(me + d))
        def _():
            coef_copy(i, d).wait_send()
    for level in range(3):
        for slot in range(4):
            @pl.when(goes(level, slot))
            def _():
                for c in range(CHIPS[level]):
                    up_copy(level, slot, c).wait_send()


def on_device(vectors, leaf_basis, near_blocks, near_index, near_count, leaf_couple, far_index, leaf_transfer, level_couple, level_transfer):
    hbm = pl.BlockSpec(memory_space=pltpu.HBM)
    dma = pltpu.SemaphoreType.DMA
    return pl.pallas_call(
        kernel,
        out_shape=jax.ShapeDtypeStruct((4, 32, 256), F32),
        in_specs=[hbm] * 10,
        out_specs=pl.BlockSpec(memory_space=pltpu.VMEM),
        scratch_shapes=[
            pltpu.VMEM((20, 32, 256), BF16),
            pltpu.VMEM((4, 64, 256), BF16),
            pltpu.VMEM((4, 3, 256, 256), BF16),
            pltpu.VMEM((4, 6, 64, 64), BF16),
            pltpu.VMEM((4, 64, 64), BF16),
            pltpu.VMEM((3, 1, 4, 64, 64), BF16),
            pltpu.VMEM((2, 1, 64, 64), BF16),
            pltpu.VMEM((5, 32, 256), BF16),
            pltpu.VMEM((20, 32, 128), BF16),
            pltpu.VMEM((3, 16, 128), BF16),
            pltpu.VMEM((16, 16, 128), BF16),
            pltpu.VMEM((2, 3, 256, 256), BF16),
            pltpu.VMEM((2, 2, 16, 128), BF16),
            pltpu.SMEM((4, 3), jnp.int32),
            pltpu.SMEM((4,), jnp.int32),
            pltpu.SMEM((4, 6), jnp.int32),
            dma((10,)), dma((4,)), dma((4,)), dma((4,)), dma((4,)), dma((16,)), dma((16,)), dma((2,)), pltpu.SemaphoreType.REGULAR((2,)),
        ],
        compiler_params=pltpu.CompilerParams(
            collective_id=0, has_side_effects=True, vmem_limit_bytes=32 * 2**20),
        name="h2_product",
    )(*(pltpu.with_memory_space_constraint(x, pltpu.HBM) for x in (near_index, near_count, far_index, vectors, jnp.swapaxes(leaf_basis, 1, 2), near_blocks, leaf_couple, leaf_transfer, level_couple, level_transfer)))


def solution(mesh):
    dim = P(("gx", "gy"))
    in_specs = (dim, dim, dim, dim, dim, dim, dim, dim, P(None, ("gx", "gy")), P(None, ("gx", "gy")))
    return jax.shard_map(on_device, mesh=mesh, in_specs=in_specs, out_specs=dim, check_vma=False)
```

```python
import jax
import jax.numpy as jnp
from jax import lax
from jax.experimental import pallas as pl
from jax.experimental.pallas import tpu as pltpu
from jax.sharding import PartitionSpec as P

MESH = pl.DeviceIdType.MESH
NODES = 512
OFFSETS = (-3, -2, 2, 3)
F32, BF16 = jnp.float32, jnp.bfloat16


def split(x):
    high = x.astype(BF16)
    return high, (x - high.astype(F32)).astype(BF16)


def dot(a, b):
    return jnp.dot(a, b, preferred_element_type=F32)


def dot_t(a, b):
    return lax.dot_general(a, b, (((1,), (1,)), ((), ())), preferred_element_type=F32)


def twice(dot_fn, x, w):
    rows = x.shape[0]
    both = dot_fn(jnp.concatenate(split(x), axis=0), w)
    return both[:rows] + both[rows:]


def packed(x):
    x = x.astype(BF16)
    return jnp.concatenate([x[:16], x[16:]], axis=1)


def where_is(index):
    return (jnp.right_shift(index, 5), jnp.bitwise_and(index, 31))


FIRST = (0, 4, 8)
CHIPS = (1, 1, 2)


def both(a, b):
    return jnp.logical_and(a, b)


def kernel(
    near_index_hbm, near_count_hbm, far_index_hbm,
    vectors_hbm, basis_hbm, near_hbm, couple_hbm, transfer_hbm, lcouple_hbm, ltransfer_hbm,
    out_ref,
    window, basis, blocks, couple, transfer, lcouple, ltransfer,
    coeffs, doubled, ups, arrived, weights, halves, near_index, near_count, far_index,
    load_sem, vec_send, vec_recv, coef_send, coef_recv, up_send, up_recv, swap_sem, known,
):
    me = lax.axis_index("gx") * 32 + lax.axis_index("gy")

    def inside(device):
        return jnp.logical_and(device >= 0, device < NODES)

    barrier = pltpu.get_barrier_semaphore()

    def tell(semaphore, distances):
        count = jnp.int32(0)
        for d in distances:
            there = inside(me + d)
            count = count + (both(there, me + d != 0) if d < 0 else there).astype(jnp.int32)
            if d > 0 or semaphore is not barrier:
                there = both(there, (me if d > 0 else me + d) != 0)

            @pl.when(there)
            def _():
                pl.semaphore_signal(semaphore, inc=1, device_id=where_is(me + d), device_id_type=MESH)

        return count

    beside = tell(barrier, (-8, 8, -6, 6, -4, 4, -3, 3, -2, 2, -1, 1))

    loads = [
        pltpu.make_async_copy(source, target, load_sem.at[i])
        for i, (source, target) in enumerate((
            (vectors_hbm, window.at[pl.ds(8, 4)]),
            (basis_hbm, basis),
            (transfer_hbm, transfer),
            (ltransfer_hbm, ltransfer),
            (lcouple_hbm, lcouple),
            (couple_hbm, couple),
            (near_hbm, blocks),
            (near_index_hbm, near_index),
            (near_count_hbm, near_count),
            (far_index_hbm, far_index),
        ))
    ]
    for load in loads[:4]:
        load.start()

    for level in range(3):
        members = 2**level
        cluster = jnp.right_shift(me, level)
        for slot, offset in enumerate(OFFSETS):
            source = cluster + offset

            @pl.when(jnp.logical_or(source < 0, source >= NODES // members))
            def _():
                for c in range(CHIPS[level]):
                    arrived[FIRST[level] + slot * CHIPS[level] + c] = jnp.zeros((16, 128), BF16)

    side = 2 * jnp.bitwise_and(me, 1) - 1

    def vec_copy(role):
        to = (me + side, me - 2 * side, me - side, me - side)[role]
        block = (2 - side, 2 + 2 * side, 2 + side, 2 + 2 * side)[role]
        mine = 2 + side if role == 3 else 2
        return pltpu.make_async_remote_copy(
            src_ref=window.at[pl.ds(mine * 4, 4)], dst_ref=window.at[pl.ds(block * 4, 4)],
            send_sem=vec_send.at[role], recv_sem=vec_recv.at[role],
            device_id=where_is(to), device_id_type=MESH)

    vec_goes = [inside(me + side), inside(me - 2 * side), inside(me - side), inside(me + side)]
    not_first = [me + side != 0, me - 2 * side != 0, me - side != 0]
    vec_comes = [inside(me + side), inside(me + 2 * side), inside(me - side), inside(me - 2 * side)]

    def coef_copy(role):
        to = (me + side, me - 2 * side, me - side, me - side)[role]
        block = (2 - side, 2 + 2 * side, 2 + side, 2 + 2 * side)[role]
        return pltpu.make_async_remote_copy(
            src_ref=coeffs.at[2 + side if role == 3 else 2], dst_ref=coeffs.at[block],
            send_sem=coef_send.at[role], recv_sem=coef_recv.at[role],
            device_id=where_is(to), device_id_type=MESH)

    core, chip = jnp.bitwise_and(me, 1), jnp.bitwise_and(jnp.right_shift(me, 1), 1)

    def up_target(level, slot, c):
        if level == 2:
            return (jnp.right_shift(me, 2) - OFFSETS[slot]) * 4 + 2 * c + core
        return me - OFFSETS[slot] * 2**level

    def up_copy(level, slot, c):
        first = FIRST[level] + slot * CHIPS[level]
        to, mine = up_target(level, slot, c), first + chip if level == 2 else first
        return pltpu.make_async_remote_copy(
            src_ref=ups.at[level], dst_ref=arrived.at[mine],
            send_sem=up_send.at[first + c], recv_sem=up_recv.at[mine],
            device_id=where_is(to), device_id_type=MESH)

    def arrival(level, slot, c):
        place = FIRST[level] + slot * CHIPS[level] + c
        return pltpu.make_async_remote_copy(
            src_ref=ups.at[level], dst_ref=arrived.at[place],
            send_sem=up_send.at[place], recv_sem=up_recv.at[place],
            device_id=where_is(jnp.bitwise_and(me + 1, NODES - 1)), device_id_type=MESH)

    swap = pltpu.make_async_remote_copy(
        src_ref=halves.at[0], dst_ref=halves.at[1], send_sem=swap_sem.at[0], recv_sem=swap_sem.at[1],
        device_id=where_is(jnp.bitwise_xor(me, 1)), device_id_type=MESH)

    def goes(level, slot):
        to = jnp.right_shift(me, level) - OFFSETS[slot]
        return both(to >= 0, to < NODES // 2**level)

    def comes(level, slot):
        source = jnp.right_shift(me, level) + OFFSETS[slot]
        return both(source >= 0, source < NODES // 2**level)

    def send_up(level, slot):
        @pl.when(goes(level, slot))
        def _():
            for c in range(CHIPS[level]):
                if OFFSETS[slot] > 0 and c == 0:
                    pl.when(up_target(level, slot, c) != 0)(up_copy(level, slot, c).start)
                else:
                    up_copy(level, slot, c).start()

    for load in loads[:4]:
        load.wait()
    for load in loads[4:]:
        load.start()
    own = [dot_t(window[8 + t], basis[t]).astype(BF16) for t in range(4)]
    coefficients = jnp.concatenate(own, axis=1)
    coeffs[2] = coefficients
    up0 = dot(coefficients, transfer[...].reshape(256, 64))
    up1 = twice(dot, up0, ltransfer[0, 0])
    ups[0] = packed(up0)
    half = jnp.concatenate([up1[:16], up1[16:]], axis=1)
    high, low = split(half)
    halves[0, 0] = high
    halves[0, 1] = low

    pl.semaphore_wait(barrier, beside)
    below = tell(known.at[1], (-8,))
    above = tell(known.at[0], (8,))

    @pl.when(me == 0)
    def _():
        for device in (1, 2, 3, 4, 6, 8):
            pl.semaphore_signal(known.at[2], inc=1, device_id=where_is(jnp.int32(device)), device_id_type=MESH)

    pl.when(me != 1)(swap.start)
    for role in range(3):
        pl.when(both(vec_goes[role], not_first[role]))(coef_copy(role).start)
    for slot in range(4):
        send_up(0, slot)
    for role in range(3):
        pl.when(both(vec_goes[role], not_first[role]))(vec_copy(role).start)

    @pl.when(me == 1)
    def _():
        pl.semaphore_wait(known.at[2], 1)
        swap.start()
        coef_copy(2).start()
        vec_copy(2).start()

    swap.wait_recv()
    half = half + (halves[1, 0].astype(F32) + halves[1, 1].astype(F32))
    ups[1] = half.astype(BF16)
    turned = pltpu.roll(half, 64, 1)
    pair = jnp.concatenate([half, turned], axis=0)[:, :64]
    ups[2] = packed(twice(dot, pair, ltransfer[1, 0]))
    for slot in range(4):
        send_up(1, slot)

    def send_two_off(slot, c, close):
        reached = (c <= chip) if slot == 1 else (c >= chip)
        if c == slot - 1:
            if not close:
                return
            reached = True
        elif not close:
            reached = jnp.logical_not(reached)
        reached = both(reached, up_target(2, slot, c) != 0)
        pl.when(both(goes(2, slot), reached))(up_copy(2, slot, c).start)

    def to_above():
        @pl.when(above > 0)
        def _():
            pl.semaphore_wait(known.at[1], above)

        send_up(2, 0)
        send_two_off(1, 1, False)

    for slot in (1, 2):
        for c in range(2):
            send_two_off(slot, c, True)
    rising = jnp.bitwise_and(jnp.right_shift(me, 2), 7) < 4
    pl.when(rising)(to_above)

    @pl.when(below > 0)
    def _():
        pl.semaphore_wait(known.at[0], below)

    send_up(2, 3)
    send_two_off(2, 0, False)
    pl.when(jnp.logical_not(rising))(to_above)

    @pl.when(both(both(me >= 2, me <= 14), jnp.logical_or(core == 0, me == 3)))
    def _():
        pl.semaphore_wait(known.at[2], 1)

        @pl.when(both(both(me >= 2, me <= 6), core == 0))
        def _():
            pl.semaphore_signal(known.at[2], inc=1, device_id=where_is(me + 8), device_id_type=MESH)

        @pl.when(me == 8)
        def _():
            pl.semaphore_signal(known.at[1], inc=1, device_id=where_is(jnp.int32(0)), device_id_type=MESH)

        for level in range(3):
            for slot in (2, 3):
                pl.when(up_target(level, slot, 0) == 0)(up_copy(level, slot, 0).start)


    loads[4].wait()
    transfer_all = transfer[...].reshape(256, 64)
    step = lcouple[0, 0].reshape(256, 64)
    mats = [step.astype(F32)]
    mats.append(dot_t(lcouple[1, 0].reshape(256, 64), ltransfer[0, 0]))
    mats.append(twice(dot_t, dot_t(lcouple[2, 0].reshape(256, 64), ltransfer[1, 0]), ltransfer[0, 0]))
    for level in range(3):
        high, low = split(twice(dot_t, mats[level], transfer_all))
        weights[0, level] = high
        weights[1, level] = low

    lane = lax.broadcasted_iota(jnp.int32, (32, 128), 1)
    left = lane < 64
    left16 = left[:16]

    def level_part(level):
        sums = []
        for slot in range(4):
            place = FIRST[level] + slot * CHIPS[level]
            total = arrived[place].astype(F32)
            for c in range(1, CHIPS[level]):
                total = total + arrived[place + c].astype(F32)
            sums.append(total)
        parts = []
        for a, b in ((0, 1), (2, 3)):
            top = jnp.where(left16, sums[a], pltpu.roll(sums[b], 64, 1))
            low = jnp.where(left16, pltpu.roll(sums[a], 64, 1), sums[b])
            parts.append(jnp.concatenate([top, low], axis=0))
        high, low = split(jnp.concatenate(parts, axis=1))
        both = dot(jnp.concatenate([high, low], axis=0), weights[0, level])
        return both[:32] + both[32:] + dot(high, weights[1, level])

    def wait_level(level):
        for slot in range(4):
            @pl.when(comes(level, slot))
            def _():
                for c in range(CHIPS[level]):
                    arrival(level, slot, c).wait_recv()

    @pl.when(vec_comes[0])
    def _():
        coef_copy(0).wait_recv()
        coef_copy(3).start()
        vec_copy(0).wait_recv()
        vec_copy(3).start()

    for role in range(1, 4):
        pl.when(vec_comes[role])(coef_copy(role).wait_recv)

    loads[5].wait()
    loads[9].wait()
    for block in range(5):
        for pair in range(2):
            two = coeffs[block, :, pl.ds(pair * 128, 128)].astype(F32)
            turned = pltpu.roll(two, 64, 1)
            doubled[block * 4 + pair * 2] = jnp.where(left, two, turned).astype(BF16)
            doubled[block * 4 + pair * 2 + 1] = jnp.where(left, turned, two).astype(BF16)
    base = (me - 2) * 4

    def place(leaf):
        return jnp.clip(leaf - base, 0, 19)

    local = []
    for t in range(4):
        cols = []
        for j in range(0, 6, 2):
            first = doubled[place(far_index[t, j])]
            second = doubled[place(far_index[t, j + 1])]
            cols.append(jnp.where(left, first, second))
        local.append(dot(jnp.concatenate(cols, axis=1), couple[t].reshape(384, 64)))
    field = jnp.concatenate(local, axis=1)

    wait_level(0)
    field = field + level_part(0)

    def all_sent(level):
        for slot in range(4):
            @pl.when(goes(level, slot))
            def _():
                for c in range(CHIPS[level]):
                    up_copy(level, slot, c).wait_send()

    swap.wait_send()
    for role in range(4):
        pl.when(vec_goes[role])(coef_copy(role).wait_send)
    all_sent(0)
    all_sent(1)
    for role in range(3):
        pl.when(vec_goes[role])(vec_copy(role).wait_send)

    loads[6].wait()
    loads[7].wait()
    loads[8].wait()
    for role in range(1, 4):
        pl.when(vec_comes[role])(vec_copy(role).wait_recv)
    for t in range(4):
        picked = []
        for j in range(3):
            rows = window[place(near_index[t, j])]
            picked.append(jnp.where(j < near_count[t], rows, jnp.zeros_like(rows)))
        out_ref[t] = dot(jnp.concatenate(picked, axis=1), blocks[t].reshape(768, 256))

    wait_level(1)
    field = field + level_part(1)
    wait_level(2)
    field = (field + level_part(2)).astype(BF16)
    for t in range(4):
        out_ref[t] = out_ref[t] + dot(field[:, t * 64:(t + 1) * 64], basis[t])

    pl.when(vec_goes[3])(vec_copy(3).wait_send)
    all_sent(2)


def on_device(vectors, leaf_basis, near_blocks, near_index, near_count, leaf_couple, far_index, leaf_transfer, level_couple, level_transfer):
    hbm = pl.BlockSpec(memory_space=pltpu.HBM)
    dma = pltpu.SemaphoreType.DMA
    return pl.pallas_call(
        kernel,
        out_shape=jax.ShapeDtypeStruct((4, 32, 256), F32),
        in_specs=[hbm] * 10,
        out_specs=pl.BlockSpec(memory_space=pltpu.VMEM),
        scratch_shapes=[
            pltpu.VMEM((20, 32, 256), BF16),
            pltpu.VMEM((4, 64, 256), BF16),
            pltpu.VMEM((4, 3, 256, 256), BF16),
            pltpu.VMEM((4, 6, 64, 64), BF16),
            pltpu.VMEM((4, 64, 64), BF16),
            pltpu.VMEM((3, 1, 4, 64, 64), BF16),
            pltpu.VMEM((2, 1, 64, 64), BF16),
            pltpu.VMEM((5, 32, 256), BF16),
            pltpu.VMEM((20, 32, 128), BF16),
            pltpu.VMEM((3, 16, 128), BF16),
            pltpu.VMEM((16, 16, 128), BF16),
            pltpu.VMEM((2, 3, 256, 256), BF16),
            pltpu.VMEM((2, 2, 16, 128), BF16),
            pltpu.SMEM((4, 3), jnp.int32),
            pltpu.SMEM((4,), jnp.int32),
            pltpu.SMEM((4, 6), jnp.int32),
            dma((10,)), dma((4,)), dma((4,)), dma((4,)), dma((4,)), dma((16,)), dma((16,)), dma((2,)), pltpu.SemaphoreType.REGULAR((3,)),
        ],
        compiler_params=pltpu.CompilerParams(
            collective_id=0, has_side_effects=True, vmem_limit_bytes=32 * 2**20),
        name="h2_product",
    )(*(pltpu.with_memory_space_constraint(x, pltpu.HBM) for x in (near_index, near_count, far_index, vectors, jnp.swapaxes(leaf_basis, 1, 2), near_blocks, leaf_couple, leaf_transfer, level_couple, level_transfer)))


def solution(mesh):
    dim = P(("gx", "gy"))
    in_specs = (dim, dim, dim, dim, dim, dim, dim, dim, P(None, ("gx", "gy")), P(None, ("gx", "gy")))
    return jax.shard_map(on_device, mesh=mesh, in_specs=in_specs, out_specs=dim, check_vma=False)
```

```python
import jax
import jax.numpy as jnp
from jax import lax
from jax.experimental import pallas as pl
from jax.experimental.pallas import tpu as pltpu
from jax.sharding import PartitionSpec as P

MESH = pl.DeviceIdType.MESH
NODES = 512
OFFSETS = (-3, -2, 2, 3)
F32, BF16 = jnp.float32, jnp.bfloat16


def split(x):
    high = x.astype(BF16)
    return high, (x - high.astype(F32)).astype(BF16)


def dot(a, b):
    return jnp.dot(a, b, preferred_element_type=F32)


def dot_t(a, b):
    return lax.dot_general(a, b, (((1,), (1,)), ((), ())), preferred_element_type=F32)


def twice(dot_fn, x, w):
    rows = x.shape[0]
    both = dot_fn(jnp.concatenate(split(x), axis=0), w)
    return both[:rows] + both[rows:]


def packed(x):
    x = x.astype(BF16)
    return jnp.concatenate([x[:16], x[16:]], axis=1)


def where_is(index):
    return (jnp.right_shift(index, 5), jnp.bitwise_and(index, 31))


FIRST = (0, 4, 8)
CHIPS = (1, 1, 2)


def both(a, b):
    return jnp.logical_and(a, b)


def kernel(
    near_index_hbm, near_count_hbm, far_index_hbm,
    vectors_hbm, basis_hbm, near_hbm, couple_hbm, transfer_hbm, lcouple_hbm, ltransfer_hbm,
    out_ref,
    window, basis, blocks, couple, transfer, lcouple, ltransfer,
    coeffs, doubled, ups, arrived, weights, halves, near_index, near_count, far_index,
    load_sem, vec_send, vec_recv, coef_send, coef_recv, up_send, up_recv, swap_sem, known,
):
    me = lax.axis_index("gx") * 32 + lax.axis_index("gy")

    def inside(device):
        return jnp.logical_and(device >= 0, device < NODES)

    barrier = pltpu.get_barrier_semaphore()

    def one_row(a, b):
        return jnp.right_shift(me + a, 5) == jnp.right_shift(me + b, 5)

    def tell(semaphore, distances, when=True, comes_when=True):
        count = jnp.int32(0)
        for d in distances:
            there = inside(me + d)
            count = count + both(both(there, me + d != 0) if d < 0 else there, comes_when).astype(jnp.int32)
            there = both(there, when)
            if d > 0 or semaphore is not barrier:
                there = both(there, (me if d > 0 else me + d) != 0)

            @pl.when(there)
            def _():
                pl.semaphore_signal(semaphore, inc=1, device_id=where_is(me + d), device_id_type=MESH)

        return count

    beside = tell(barrier, (-8, 8, -6, 6, -4, 4, -3, 3, -2, 2, -1, 1))

    loads = [
        pltpu.make_async_copy(source, target, load_sem.at[i])
        for i, (source, target) in enumerate((
            (vectors_hbm, window.at[pl.ds(8, 4)]),
            (basis_hbm, basis),
            (transfer_hbm, transfer),
            (ltransfer_hbm, ltransfer),
            (lcouple_hbm, lcouple),
            (couple_hbm, couple),
            (near_hbm, blocks),
            (near_index_hbm, near_index),
            (near_count_hbm, near_count),
            (far_index_hbm, far_index),
        ))
    ]
    for load in loads[:4]:
        load.start()

    for level in range(3):
        members = 2**level
        cluster = jnp.right_shift(me, level)
        for slot, offset in enumerate(OFFSETS):
            source = cluster + offset

            @pl.when(jnp.logical_or(source < 0, source >= NODES // members))
            def _():
                for c in range(CHIPS[level]):
                    arrived[FIRST[level] + slot * CHIPS[level] + c] = jnp.zeros((16, 128), BF16)

    side = 2 * jnp.bitwise_and(me, 1) - 1

    def vec_copy(role):
        to = (me + side, me - 2 * side, me - side, me - side)[role]
        block = (2 - side, 2 + 2 * side, 2 + side, 2 + 2 * side)[role]
        mine = 2 + side if role == 3 else 2
        return pltpu.make_async_remote_copy(
            src_ref=window.at[pl.ds(mine * 4, 4)], dst_ref=window.at[pl.ds(block * 4, 4)],
            send_sem=vec_send.at[role], recv_sem=vec_recv.at[role],
            device_id=where_is(to), device_id_type=MESH)

    vec_goes = [inside(me + side), inside(me - 2 * side), inside(me - side), inside(me + side)]
    not_first = [me + side != 0, me - 2 * side != 0, me - side != 0]
    vec_comes = [inside(me + side), inside(me + 2 * side), inside(me - side), inside(me - 2 * side)]

    def coef_copy(role):
        to = (me + side, me - 2 * side, me - side, me - side)[role]
        block = (2 - side, 2 + 2 * side, 2 + side, 2 + 2 * side)[role]
        return pltpu.make_async_remote_copy(
            src_ref=coeffs.at[2 + side if role == 3 else 2], dst_ref=coeffs.at[block],
            send_sem=coef_send.at[role], recv_sem=coef_recv.at[role],
            device_id=where_is(to), device_id_type=MESH)

    core, chip = jnp.bitwise_and(me, 1), jnp.bitwise_and(jnp.right_shift(me, 1), 1)

    def up_target(level, slot, c):
        if level == 2:
            return (jnp.right_shift(me, 2) - OFFSETS[slot]) * 4 + 2 * c + core
        return me - OFFSETS[slot] * 2**level

    def up_copy(level, slot, c):
        first = FIRST[level] + slot * CHIPS[level]
        to, mine = up_target(level, slot, c), first + chip if level == 2 else first
        return pltpu.make_async_remote_copy(
            src_ref=ups.at[level], dst_ref=arrived.at[mine],
            send_sem=up_send.at[first + c], recv_sem=up_recv.at[mine],
            device_id=where_is(to), device_id_type=MESH)

    def arrival(level, slot, c):
        place = FIRST[level] + slot * CHIPS[level] + c
        return pltpu.make_async_remote_copy(
            src_ref=ups.at[level], dst_ref=arrived.at[place],
            send_sem=up_send.at[place], recv_sem=up_recv.at[place],
            device_id=where_is(jnp.bitwise_and(me + 1, NODES - 1)), device_id_type=MESH)

    swap = pltpu.make_async_remote_copy(
        src_ref=halves.at[0], dst_ref=halves.at[1], send_sem=swap_sem.at[0], recv_sem=swap_sem.at[1],
        device_id=where_is(jnp.bitwise_xor(me, 1)), device_id_type=MESH)

    def goes(level, slot):
        to = jnp.right_shift(me, level) - OFFSETS[slot]
        return both(to >= 0, to < NODES // 2**level)

    def comes(level, slot):
        source = jnp.right_shift(me, level) + OFFSETS[slot]
        return both(source >= 0, source < NODES // 2**level)

    def send_up(level, slot):
        @pl.when(goes(level, slot))
        def _():
            for c in range(CHIPS[level]):
                if OFFSETS[slot] > 0 and c == 0:
                    pl.when(up_target(level, slot, c) != 0)(up_copy(level, slot, c).start)
                else:
                    up_copy(level, slot, c).start()

    for load in loads[:4]:
        load.wait()
    for load in loads[4:]:
        load.start()
    own = [dot_t(window[8 + t], basis[t]).astype(BF16) for t in range(4)]
    coefficients = jnp.concatenate(own, axis=1)
    coeffs[2] = coefficients
    up0 = dot(coefficients, transfer[...].reshape(256, 64))
    up1 = twice(dot, up0, ltransfer[0, 0])
    ups[0] = packed(up0)
    half = jnp.concatenate([up1[:16], up1[16:]], axis=1)
    high, low = split(half)
    halves[0, 0] = high
    halves[0, 1] = low

    pl.semaphore_wait(barrier, beside)
    near_end, near_start = jnp.logical_not(one_row(0, 8)), jnp.logical_not(one_row(0, -8))
    below = tell(known.at[1], (-8,), one_row(0, -8), one_row(0, -8))
    below += tell(known.at[1], (-4,), jnp.logical_not(one_row(-4, 4)), near_start)
    below += tell(known.at[1], (-6,), both(chip == 1, jnp.logical_not(one_row(-6, 2))), both(chip == 1, near_start))
    above = tell(known.at[0], (8,), one_row(0, 8), one_row(0, 8))
    above += tell(known.at[0], (4,), jnp.logical_not(one_row(-4, 4)), near_end)
    above += tell(known.at[0], (6,), both(chip == 0, jnp.logical_not(one_row(6, -2))), both(chip == 0, near_end))

    @pl.when(me == 0)
    def _():
        for device in (1, 2, 3, 4, 6, 8):
            pl.semaphore_signal(known.at[2], inc=1, device_id=where_is(jnp.int32(device)), device_id_type=MESH)

    pl.when(me != 1)(swap.start)
    for role in range(3):
        pl.when(both(vec_goes[role], not_first[role]))(coef_copy(role).start)
    for slot in range(4):
        send_up(0, slot)
    for role in range(3):
        pl.when(both(vec_goes[role], not_first[role]))(vec_copy(role).start)

    @pl.when(me == 1)
    def _():
        pl.semaphore_wait(known.at[2], 1)
        swap.start()
        coef_copy(2).start()
        vec_copy(2).start()

    swap.wait_recv()
    half = half + (halves[1, 0].astype(F32) + halves[1, 1].astype(F32))
    ups[1] = half.astype(BF16)
    turned = pltpu.roll(half, 64, 1)
    pair = jnp.concatenate([half, turned], axis=0)[:, :64]
    ups[2] = packed(twice(dot, pair, ltransfer[1, 0]))
    for slot in range(4):
        send_up(1, slot)

    def send_two_off(slot, c, close):
        reached = (c <= chip) if slot == 1 else (c >= chip)
        if c == slot - 1:
            if not close:
                return
            reached = True
        elif not close:
            reached = jnp.logical_not(reached)
        reached = both(reached, up_target(2, slot, c) != 0)
        pl.when(both(goes(2, slot), reached))(up_copy(2, slot, c).start)

    def to_above():
        @pl.when(above > 0)
        def _():
            pl.semaphore_wait(known.at[1], above)

        send_up(2, 0)
        send_two_off(1, 1, False)

    for slot in (1, 2):
        for c in range(2):
            send_two_off(slot, c, True)
    rising = jnp.bitwise_and(jnp.right_shift(me, 2), 7) < 4
    pl.when(rising)(to_above)

    @pl.when(below > 0)
    def _():
        pl.semaphore_wait(known.at[0], below)

    send_up(2, 3)
    send_two_off(2, 0, False)
    pl.when(jnp.logical_not(rising))(to_above)

    @pl.when(both(both(me >= 2, me <= 14), jnp.logical_or(core == 0, me == 3)))
    def _():
        pl.semaphore_wait(known.at[2], 1)

        @pl.when(both(both(me >= 2, me <= 6), core == 0))
        def _():
            pl.semaphore_signal(known.at[2], inc=1, device_id=where_is(me + 8), device_id_type=MESH)

        @pl.when(me == 8)
        def _():
            pl.semaphore_signal(known.at[1], inc=1, device_id=where_is(jnp.int32(0)), device_id_type=MESH)

        for level in range(3):
            for slot in (2, 3):
                pl.when(up_target(level, slot, 0) == 0)(up_copy(level, slot, 0).start)


    loads[4].wait()
    transfer_all = transfer[...].reshape(256, 64)
    step = lcouple[0, 0].reshape(256, 64)
    mats = [step.astype(F32)]
    mats.append(dot_t(lcouple[1, 0].reshape(256, 64), ltransfer[0, 0]))
    mats.append(twice(dot_t, dot_t(lcouple[2, 0].reshape(256, 64), ltransfer[1, 0]), ltransfer[0, 0]))
    for level in range(3):
        high, low = split(twice(dot_t, mats[level], transfer_all))
        weights[0, level] = high
        weights[1, level] = low

    lane = lax.broadcasted_iota(jnp.int32, (32, 128), 1)
    left = lane < 64
    left16 = left[:16]

    def level_part(level):
        sums = []
        for slot in range(4):
            place = FIRST[level] + slot * CHIPS[level]
            total = arrived[place].astype(F32)
            for c in range(1, CHIPS[level]):
                total = total + arrived[place + c].astype(F32)
            sums.append(total)
        parts = []
        for a, b in ((0, 1), (2, 3)):
            top = jnp.where(left16, sums[a], pltpu.roll(sums[b], 64, 1))
            low = jnp.where(left16, pltpu.roll(sums[a], 64, 1), sums[b])
            parts.append(jnp.concatenate([top, low], axis=0))
        high, low = split(jnp.concatenate(parts, axis=1))
        both = dot(jnp.concatenate([high, low], axis=0), weights[0, level])
        return both[:32] + both[32:] + dot(high, weights[1, level])

    def wait_level(level):
        for slot in range(4):
            @pl.when(comes(level, slot))
            def _():
                for c in range(CHIPS[level]):
                    arrival(level, slot, c).wait_recv()

    @pl.when(vec_comes[0])
    def _():
        coef_copy(0).wait_recv()
        coef_copy(3).start()
        vec_copy(0).wait_recv()
        vec_copy(3).start()

    for role in range(1, 4):
        pl.when(vec_comes[role])(coef_copy(role).wait_recv)

    loads[5].wait()
    loads[9].wait()
    for block in range(5):
        for pair in range(2):
            two = coeffs[block, :, pl.ds(pair * 128, 128)].astype(F32)
            turned = pltpu.roll(two, 64, 1)
            doubled[block * 4 + pair * 2] = jnp.where(left, two, turned).astype(BF16)
            doubled[block * 4 + pair * 2 + 1] = jnp.where(left, turned, two).astype(BF16)
    base = (me - 2) * 4

    def place(leaf):
        return jnp.clip(leaf - base, 0, 19)

    local = []
    for t in range(4):
        cols = []
        for j in range(0, 6, 2):
            first = doubled[place(far_index[t, j])]
            second = doubled[place(far_index[t, j + 1])]
            cols.append(jnp.where(left, first, second))
        local.append(dot(jnp.concatenate(cols, axis=1), couple[t].reshape(384, 64)))
    field = jnp.concatenate(local, axis=1)

    wait_level(0)
    field = field + level_part(0)

    def all_sent(level):
        for slot in range(4):
            @pl.when(goes(level, slot))
            def _():
                for c in range(CHIPS[level]):
                    up_copy(level, slot, c).wait_send()

    swap.wait_send()
    for role in range(4):
        pl.when(vec_goes[role])(coef_copy(role).wait_send)
    all_sent(0)
    all_sent(1)
    for role in range(3):
        pl.when(vec_goes[role])(vec_copy(role).wait_send)

    loads[6].wait()
    loads[7].wait()
    loads[8].wait()
    for role in range(1, 4):
        pl.when(vec_comes[role])(vec_copy(role).wait_recv)
    for t in range(4):
        picked = []
        for j in range(3):
            rows = window[place(near_index[t, j])]
            picked.append(jnp.where(j < near_count[t], rows, jnp.zeros_like(rows)))
        out_ref[t] = dot(jnp.concatenate(picked, axis=1), blocks[t].reshape(768, 256))

    wait_level(1)
    field = field + level_part(1)
    wait_level(2)
    field = (field + level_part(2)).astype(BF16)
    for t in range(4):
        out_ref[t] = out_ref[t] + dot(field[:, t * 64:(t + 1) * 64], basis[t])

    pl.when(vec_goes[3])(vec_copy(3).wait_send)
    all_sent(2)


def on_device(vectors, leaf_basis, near_blocks, near_index, near_count, leaf_couple, far_index, leaf_transfer, level_couple, level_transfer):
    hbm = pl.BlockSpec(memory_space=pltpu.HBM)
    dma = pltpu.SemaphoreType.DMA
    return pl.pallas_call(
        kernel,
        out_shape=jax.ShapeDtypeStruct((4, 32, 256), F32),
        in_specs=[hbm] * 10,
        out_specs=pl.BlockSpec(memory_space=pltpu.VMEM),
        scratch_shapes=[
            pltpu.VMEM((20, 32, 256), BF16),
            pltpu.VMEM((4, 64, 256), BF16),
            pltpu.VMEM((4, 3, 256, 256), BF16),
            pltpu.VMEM((4, 6, 64, 64), BF16),
            pltpu.VMEM((4, 64, 64), BF16),
            pltpu.VMEM((3, 1, 4, 64, 64), BF16),
            pltpu.VMEM((2, 1, 64, 64), BF16),
            pltpu.VMEM((5, 32, 256), BF16),
            pltpu.VMEM((20, 32, 128), BF16),
            pltpu.VMEM((3, 16, 128), BF16),
            pltpu.VMEM((16, 16, 128), BF16),
            pltpu.VMEM((2, 3, 256, 256), BF16),
            pltpu.VMEM((2, 2, 16, 128), BF16),
            pltpu.SMEM((4, 3), jnp.int32),
            pltpu.SMEM((4,), jnp.int32),
            pltpu.SMEM((4, 6), jnp.int32),
            dma((10,)), dma((4,)), dma((4,)), dma((4,)), dma((4,)), dma((16,)), dma((16,)), dma((2,)), pltpu.SemaphoreType.REGULAR((3,)),
        ],
        compiler_params=pltpu.CompilerParams(
            collective_id=0, has_side_effects=True, vmem_limit_bytes=32 * 2**20),
        name="h2_product",
    )(*(pltpu.with_memory_space_constraint(x, pltpu.HBM) for x in (near_index, near_count, far_index, vectors, jnp.swapaxes(leaf_basis, 1, 2), near_blocks, leaf_couple, leaf_transfer, level_couple, level_transfer)))


def solution(mesh):
    dim = P(("gx", "gy"))
    in_specs = (dim, dim, dim, dim, dim, dim, dim, dim, P(None, ("gx", "gy")), P(None, ("gx", "gy")))
    return jax.shard_map(on_device, mesh=mesh, in_specs=in_specs, out_specs=dim, check_vma=False)
```
